256 devices in a mesh: lang: 16 (over z_hi, x, core), seq: 16 (over y, z_lo).
Axes of the slice: x: 4, y: 4, z: 8 (z_hi: 2, z_lo: 4; z = z_hi * 4 + z_lo), core: 2. Of those that a mesh axis runs over, the one named last changes fastest.
Arguments:
- prompt_rows: bfloat16 [32768, 2048], P(('lang', 'seq')), may hold values from -6 to 6
- expert_ids: int32 [32768, 2], P(('lang', 'seq')), may hold values from 0 to 15, all different within a row; in each aligned block of 128 rows (0 to 127, 128 to 255, ...) at most 24 rows name the same one
- expert_gates: float32 [32768, 2], P(('lang', 'seq')), may hold values from 0.25 to 1
- w_gate: bfloat16 [16, 2048, 704], P('lang', 'seq'), may hold values from -0.125 to 0.125
- w_up: bfloat16 [16, 2048, 704], P('lang', 'seq'), may hold values from -0.125 to 0.125
- w_down: bfloat16 [16, 704, 2048], P('lang', None, 'seq'), may hold values from -0.21875 to 0.21875
- w_kv: bfloat16 [2048, 2, 2048], P(None, None, 'seq'), may hold values from -0.125 to 0.125
- prompt_lengths: int32 [32], P('lang'), may hold values from 256 to 1024, as said below
- latent_q: bfloat16 [32, 1024, 2048], P('lang', 'seq'), may hold values from -5 to 5
- latent_k: bfloat16 [32, 1024, 2048], P('lang', 'seq'), may hold values from -5 to 5
- latent_v: bfloat16 [32, 1024, 2048], P('lang', 'seq'), may hold values from -6 to 6
- grad_out: bfloat16 [32, 1024, 2048], P('lang', 'seq'), may hold values from -6 to 6
Outputs:
- attended: bfloat16 [32, 1024, 2048], P('lang', 'seq')
- grad_latent: bfloat16 [3, 32, 1024, 2048], P(None, 'lang', 'seq')
- grad_wkv: float32 [2048, 2, 2048], P(None, None, 'seq')
The draws below stay inside these ranges and needn't reach their ends.
Inputs may be any that keep to these rules, and one draw needn't show every extreme that they name: `expert_ids`: in each aligned block of 128 rows (the rows of one device) no expert is named by more than 24 rows. `prompt_lengths`: the first of each group of 2 pages uses its whole prompt.
All inputs are finite; a program needn't handle non-finite values.
Results may differ from the reference program's by a relative error of at most 0.03.
Values may be sent and summed in bfloat16 or wider, within the bound.
A program may use at most 128 MiB of HBM per device.

```python
import math
import jax
import jax.numpy as jnp
import numpy as np
from jax import lax

D = 2048
FF = 704
HD = 128
TOP = 2
PAGES = 2
PROMPT_DEV = 128
EXPERTS = 16
CAP = 24
HEADS = 16
PROMPT = 1024
LAT = 1024
PAGE_ALL = 32
PTOK = 32768
N_LANG = 16


def draw_latent_q(key, part):
    key = jax.random.fold_in(key, 3)
    shape = (PAGES * N_LANG, LAT, HEADS * HD)
    base = jnp.clip(jax.random.normal(key, shape, jnp.float32), -5.0, 5.0)
    return base.astype(jnp.bfloat16)


def draw_latent_k(key, part):
    key = jax.random.fold_in(key, 5)
    shape = (PAGES * N_LANG, LAT, HEADS * HD)
    base = jnp.clip(jax.random.normal(key, shape, jnp.float32), -5.0, 5.0)
    return base.astype(jnp.bfloat16)


def draw_prompt_lengths(key, part):
    key = jax.random.fold_in(key, 7)
    page_count = PAGES * N_LANG
    lengths = jax.random.randint(key, (page_count,), PROMPT // 4, PROMPT + 1, dtype=jnp.int32)
    page_index = jnp.arange(page_count, dtype=jnp.int32)
    lengths = jnp.where(page_index % PAGES == 0, PROMPT, lengths)
    lengths = jnp.where(page_index == 1, PROMPT // 4, lengths)
    return lengths.astype(jnp.int32)


def steps_of(stream_key, dims, cuts, low, high):
    def one(axis_at, shards_of):
        draws = jax.random.uniform(jax.random.fold_in(jax.random.fold_in(stream_key, 6), axis_at), (shards_of,), jnp.float32, low / len(cuts), high / len(cuts))
        return jnp.repeat(jnp.exp(draws), dims[axis_at] // shards_of).reshape((-1,) + (1,) * (len(dims) - axis_at - 1))

    gain = one(*cuts[0])
    for cut in cuts[1:]:
        gain = gain * one(*cut)
    return gain


def shared_out(rng, own, number, rows, count, top, most, slope):
    order = jax.random.permutation(rng, count)
    crowded, usual = portions_of(count, rows * top, most, slope, True), portions_of(count, rows * top, most, slope, False)
    places = jnp.arange(count)

    def named(sizes, turn):
        used = int((sizes > 0).sum())
        fixed = max(1, used // 4)
        moved = fixed + (places - fixed + turn * (used - fixed)) % max(1, count - fixed)
        return jnp.zeros((count,), jnp.int32).at[order[jnp.where(places < fixed, places, moved)]].set(jnp.asarray(sizes, jnp.int32))

    sizes = jnp.where(number % 4 == 0, named(crowded, number // 4), named(usual, number - number // 4 - 1))
    mixed = jax.random.permutation(jax.random.fold_in(own, 3), count)
    source_of, receiver = mixed[0:count // 2 * 2:2], mixed[1:count // 2 * 2:2]
    room = jnp.minimum(sizes[source_of] - 1, most - sizes[receiver]) // 2
    room = jnp.where((source_of == order[0]) | (receiver == order[0]) | (sizes[receiver] == 0), 0, jnp.maximum(room, 0))
    moved = jax.random.randint(jax.random.fold_in(own, 4), (count // 2,), 0, 1 << 20) % (room + 1)
    sizes = sizes.at[source_of].add(-moved).at[receiver].add(moved)
    members = jnp.searchsorted(jnp.cumsum(sizes), jnp.arange(rows * top), side="right").astype(jnp.int32)
    listing = members.reshape(top, rows).T
    listing = listing[jax.random.permutation(jax.random.fold_in(own, 1), rows)]
    turn = jax.random.randint(jax.random.fold_in(own, 2), (rows, 1), 0, top)
    return jnp.take_along_axis(listing, (jnp.arange(top)[None, :] + turn) % top, axis=1)


def portions_of(number_of, total, limit, lean, full):
    loads = [(1 << 20) // math.isqrt(grade ** lean) + 1 for grade in range(1, number_of + 1)]
    largest = limit if full else min(limit, max(-(-total // number_of), total * loads[0] // sum(loads)))
    least = 1 if total - largest >= number_of - 1 else 0
    given, surplus = [largest] + [least] * (number_of - 1), total - largest - least * (number_of - 1)
    while surplus > 0:
        candidates = [i for i in range(1, number_of) if given[i] < largest] or [i for i in range(1, number_of) if given[i] < limit]
        mass, budget = sum([loads[i] for i in candidates]), surplus
        for i in candidates:
            addition = min(limit - given[i], max(1, budget * loads[i] // mass), surplus)
            given[i] = given[i] + addition
            surplus = surplus - addition
    return np.array(given)


def normal_values(own_key, extent, spread, reach, pieces=(), kind=jnp.bfloat16):
    drawn = jax.random.normal(own_key, extent, jnp.float32) * spread
    if len(pieces) > 0:
        drawn = steps_of(own_key, extent, pieces, -0.22, 0.18) * drawn
    return jnp.clip(drawn, min=-reach, max=reach).astype(kind)


def setup_inputs(seed: int = 0) -> dict:
    seeds = jax.random.split(jax.random.key(seed), 13)
    prompt_rows = normal_values(seeds[0], (PTOK, D), 1.0, 6.0, ((0, 256),))
    expert_ids_keys = jax.random.split(jax.random.fold_in(seeds[1], 1), PTOK // PROMPT_DEV)
    expert_ids_turns = jax.random.permutation(jax.random.fold_in(seeds[1], 3), PTOK // PROMPT_DEV)
    expert_ids = jax.vmap(lambda own, number: shared_out(jax.random.fold_in(seeds[1], 2), own, number, PROMPT_DEV, EXPERTS, TOP, CAP, 2))(expert_ids_keys, expert_ids_turns).reshape((PTOK, TOP))
    expert_gates = jnp.clip(jnp.exp(math.log(1.0) - 1.3862944 * jax.random.uniform(seeds[2], (PTOK, TOP), jnp.float32) ** steps_of(seeds[2], (PTOK, TOP), ((0, 256),), -0.2, 0.2)), 0.25, 1.0)
    w_gate = normal_values(seeds[3], (EXPERTS, D, FF), D ** -0.5, 0.125, ((0, 16), (1, 16)))
    w_up = normal_values(seeds[4], (EXPERTS, D, FF), D ** -0.5, 0.125, ((0, 16), (1, 16)))
    w_down = normal_values(seeds[5], (EXPERTS, FF, D), FF ** -0.5, 0.21875, ((0, 16), (2, 16)))
    w_kv = normal_values(seeds[6], (D, 2, HEADS * HD), D ** -0.5, 0.125, ((2, 16),))
    prompt_lengths = draw_prompt_lengths(jax.random.fold_in(seeds[12], 71), 0)
    latent_q = draw_latent_q(jax.random.fold_in(seeds[12], 71), 0)
    latent_k = draw_latent_k(jax.random.fold_in(seeds[12], 71), 0)
    latent_v = normal_values(seeds[10], (PAGE_ALL, LAT, HEADS * HD), 1.0, 6.0, ((0, 16), (1, 16)))
    grad_out = normal_values(seeds[11], (PAGE_ALL, LAT, HEADS * HD), 1.0, 6.0, ((0, 16), (1, 16)))
    return {"prompt_rows": prompt_rows, "expert_ids": expert_ids, "expert_gates": expert_gates, "w_gate": w_gate, "w_up": w_up, "w_down": w_down, "w_kv": w_kv, "prompt_lengths": prompt_lengths, "latent_q": latent_q, "latent_k": latent_k, "latent_v": latent_v, "grad_out": grad_out}


def expert_mixture(prompt_rows, expert_ids, expert_gates, w_gate, w_up, w_down):

    def one_expert(total, expert):
        gate_proj = jnp.dot(prompt_rows, w_gate[expert], preferred_element_type=jnp.float32)
        up_proj = jnp.dot(prompt_rows, w_up[expert], preferred_element_type=jnp.float32)
        hidden = (jax.nn.silu(gate_proj) * up_proj).astype(jnp.bfloat16)
        expert_out = jnp.dot(hidden, w_down[expert], preferred_element_type=jnp.float32).astype(jnp.bfloat16)
        weighting = lax.optimization_barrier(jnp.sum(jnp.where(expert_ids == expert, expert_gates, 0.0), axis=1))
        return (total + weighting[:, None] * expert_out.astype(jnp.float32), None)
    start_total = jnp.zeros(prompt_rows.shape, jnp.float32)
    total, unused = lax.scan(one_expert, start_total, jnp.arange(w_gate.shape[0], dtype=jnp.int32))
    return total.astype(jnp.bfloat16)

def joint_attention(queries, key_rows, values, key_valid, out_grads):
    rows_all, head_size = queries.shape
    block_rows = min(512, rows_all)
    blocks = rows_all // block_rows
    score_scale = 1.0 / math.sqrt(head_size)
    query_blocks = queries.reshape(blocks, block_rows, head_size)
    grad_blocks = out_grads.reshape(blocks, block_rows, head_size)

    def one_block(carry, inputs):
        key_grad, value_grad = carry
        query_block, grad_block = inputs
        scores = lax.dot_general(query_block, key_rows, (((1,), (1,)), ((), ())), preferred_element_type=jnp.float32) * score_scale
        scores = jnp.where(key_valid[None, :], scores, -jnp.inf)
        highest = lax.optimization_barrier(jnp.max(scores, axis=1, keepdims=True))
        raised = jnp.exp(scores - highest)
        soft_weights = raised / lax.optimization_barrier(jnp.sum(raised, axis=1, keepdims=True))
        soft_low = soft_weights.astype(jnp.bfloat16)
        attended = jnp.dot(soft_low, values, preferred_element_type=jnp.float32).astype(jnp.bfloat16)
        prob_grad = lax.dot_general(grad_block, values, (((1,), (1,)), ((), ())), preferred_element_type=jnp.float32)
        centre = lax.optimization_barrier(jnp.sum(soft_weights * prob_grad, axis=1, keepdims=True))
        score_grad = (soft_weights * (prob_grad - centre) * score_scale).astype(jnp.bfloat16)
        query_grad = jnp.dot(score_grad, key_rows, preferred_element_type=jnp.float32).astype(jnp.bfloat16)
        key_grad = key_grad + lax.dot_general(score_grad, query_block, (((0,), (0,)), ((), ())), preferred_element_type=jnp.float32)
        value_grad = value_grad + lax.dot_general(soft_low, grad_block, (((0,), (0,)), ((), ())), preferred_element_type=jnp.float32)
        return ((key_grad, value_grad), (attended, query_grad))
    empty_grad = jnp.zeros(key_rows.shape, jnp.float32)
    (key_grad, value_grad), (attended, query_grad) = lax.scan(one_block, (empty_grad, empty_grad), (query_blocks, grad_blocks))
    return (attended.reshape(rows_all, head_size), query_grad.reshape(rows_all, head_size), key_grad, value_grad)

def reference(prompt_rows, expert_ids, expert_gates, w_gate, w_up, w_down, w_kv, prompt_lengths, latent_q, latent_k, latent_v, grad_out):
    mixed = expert_mixture(prompt_rows, expert_ids, expert_gates, w_gate, w_up, w_down)
    page_total = PAGES * N_LANG
    kv_flat = jnp.dot(mixed, w_kv.reshape(D, 2 * HEADS * HD), preferred_element_type=jnp.float32).astype(jnp.bfloat16)
    prompt_kv = kv_flat.reshape(page_total, PROMPT, 2, HEADS, HD)
    positions = jnp.arange(PROMPT, dtype=jnp.int32)

    def heads_first(array):
        return array.reshape(page_total, LAT, HEADS, HD).transpose(0, 2, 1, 3)

    def one_page(inputs):
        query_page, key_page, value_page, grad_page, kv_page, length = inputs
        key_valid = jnp.concatenate([jnp.ones((LAT,), bool), positions < length])
        prompt_keys = kv_page[:, 0].transpose(1, 0, 2)
        prompt_values = kv_page[:, 1].transpose(1, 0, 2)

        def one_head(head_inputs):
            query_head, key_head, value_head, grad_head, prompt_key, prompt_value = head_inputs
            key_rows = jnp.concatenate([key_head, prompt_key], axis=0)
            value_rows = jnp.concatenate([value_head, prompt_value], axis=0)
            return joint_attention(query_head, key_rows, value_rows, key_valid, grad_head)
        return lax.map(one_head, (query_page, key_page, value_page, grad_page, prompt_keys, prompt_values))
    attended, query_grad, key_grad, value_grad = lax.map(one_page, (heads_first(latent_q), heads_first(latent_k), heads_first(latent_v), heads_first(grad_out), prompt_kv, prompt_lengths))

    def rows_first(array):
        return array.transpose(0, 2, 1, 3).reshape(page_total, LAT, HEADS * HD)
    latent_key = key_grad[:, :, :LAT].astype(jnp.bfloat16)
    latent_value = value_grad[:, :, :LAT].astype(jnp.bfloat16)
    grad_latent = jnp.stack([rows_first(query_grad), rows_first(latent_key), rows_first(latent_value)])
    prompt_key = key_grad[:, :, LAT:].astype(jnp.bfloat16).transpose(0, 2, 1, 3)
    prompt_value = value_grad[:, :, LAT:].astype(jnp.bfloat16).transpose(0, 2, 1, 3)
    prompt_grad = jnp.stack([prompt_key, prompt_value], axis=2).reshape(page_total * PROMPT, 2 * HEADS * HD)
    grad_wkv = lax.dot_general(mixed, prompt_grad, (((0,), (0,)), ((), ())), preferred_element_type=jnp.float32)
    return (rows_first(attended), grad_latent, grad_wkv.reshape(D, 2, HEADS * HD))
```

```python
import functools
import math

import jax
import jax.numpy as jnp
from jax import lax
from jax.experimental import pallas as pl
from jax.experimental.pallas import tpu as pltpu
from jax.sharding import PartitionSpec as P

HD = 128
MESH = pl.DeviceIdType.MESH
ANY = pl.BlockSpec(memory_space=pl.ANY)
BF = jnp.bfloat16
F32 = jnp.float32
DMA = pltpu.SemaphoreType.DMA
ZN = 4
YN = 4


def slot_targets(expert_ids, experts_all, capacity):
    rows_local, picks = expert_ids.shape
    flat_ids = expert_ids.reshape(rows_local * picks)
    expert_range = jnp.arange(experts_all, dtype=jnp.int32)
    onehot = (flat_ids[:, None] == expert_range[None, :]).astype(jnp.int32)
    earlier = jnp.cumsum(onehot, axis=0) - onehot
    slot_index = jnp.sum(earlier * onehot, axis=1)
    return (flat_ids * capacity + slot_index).reshape(rows_local, picks)


def push(src, dst, ssem, rsem, axis, target):
    return pltpu.make_async_remote_copy(
        src_ref=src,
        dst_ref=dst,
        send_sem=ssem,
        recv_sem=rsem,
        device_id={axis: target},
        device_id_type=MESH,
    )


def greet(peers):
    barrier = pltpu.get_barrier_semaphore()
    total = 0
    for axis, targets in peers:
        if callable(targets):
            count, of = targets()

            def one(j, carry):
                pl.semaphore_signal(barrier, inc=1, device_id={axis: of(j)}, device_id_type=MESH)
                return carry

            lax.fori_loop(1, count, one, 0)
            total += count - 1
        else:
            for target in targets:
                pl.semaphore_signal(barrier, inc=1, device_id={axis: target}, device_id_type=MESH)
                total += 1
    pl.semaphore_wait(barrier, total)


def everyone(axis):
    def make():
        n = lax.axis_size(axis)
        me = lax.axis_index(axis)
        return n, lambda j: lax.rem(me + j, n)

    return make


def ring_places():
    s = lax.axis_index("seq")
    y, z = lax.div(s, ZN), lax.rem(s, ZN)
    up = lax.rem(y + 1, YN) * ZN + z
    down = lax.rem(y + YN - 1, YN) * ZN + z
    zpeers = [y * ZN + lax.rem(z + k, ZN) for k in range(1, ZN)]
    return s, y, z, up, down, zpeers


GATHER_SEMS = [DMA((ZN,))] * 10


def gather_steps(src, view, sems):
    zs, zr, us, ur, ds, dr, fus, fur, fds, fdr = sems
    s, y, z, up, down, zpeers = ring_places()
    low_y = lax.rem(y + YN - 1, YN)
    high_y = lax.rem(y + 1, YN)

    def column(k):
        return lax.rem(z + ZN - k, ZN)

    def zcopy(k):
        return push(src, view(s, None), zs.at[k], zr.at[k], "seq", zpeers[k - 1])

    def ycopies(k):
        shard = y * ZN + column(k)
        source = src if k == 0 else view(shard, None)
        return (
            push(source, view(shard, None), us.at[k], ur.at[k], "seq", up),
            push(source, view(shard, None), ds.at[k], dr.at[k], "seq", down),
        )

    def forwards(k):
        from_low = view(low_y * ZN + column(k), 0)
        from_high = view(high_y * ZN + column(k), 1)
        return (
            push(from_low, from_low, fus.at[k], fur.at[k], "seq", up),
            push(from_high, from_high, fds.at[k], fdr.at[k], "seq", down),
        )

    def pass_on(k):
        go_up, go_down = ycopies(k)
        first, second = forwards(k)
        go_up.wait_recv()
        first.start()
        go_down.wait_recv()
        second.start()

    def begin():
        for k in range(1, ZN):
            zcopy(k).start()
        for copy in ycopies(0):
            copy.start()

    def rest():
        for k in range(1, ZN):
            zcopy(k).wait_recv()
            for copy in ycopies(k):
                copy.start()
            pass_on(k - 1)
        pass_on(ZN - 1)

    def finish():
        for k in range(ZN):
            for copy in forwards(k):
                copy.wait()
            for copy in ycopies(k):
                copy.wait_send()
        for k in range(1, ZN):
            zcopy(k).wait_send()

    return begin, rest, finish


def swap_steps(axis, pieces, send, recv):
    n = lax.axis_size(axis)
    me = lax.axis_index(axis)

    def copy(i, j):
        target = lax.rem(me + j, n)
        source, landing = pieces[i]
        return push(source(target), landing(me), send.at[i, j], recv.at[i, j], axis, target)

    def begin():
        def one(j, carry):
            for i in range(len(pieces)):
                copy(i, j).start()
            return carry

        lax.fori_loop(1, n, one, 0)

    def finish():
        def one(j, carry):
            for i in range(len(pieces)):
                copy(i, j).wait()
            return carry

        lax.fori_loop(1, n, one, 0)

    return begin, finish


def dispatch_kernel(pack, outgoing, whole, arrived, send, recv, own_sem, *gsems):
    s, y, z, up, down, zpeers = ring_places()
    me = lax.axis_index("lang")

    def view(shard, half):
        columns = pl.ds(pl.multiple_of(shard * HD, HD), HD)
        if half is None:
            return whole.at[:, columns]
        rows = pack.shape[0] // 2
        return whole.at[pl.ds(half * rows, rows), columns]

    gbegin, grest, gfinish = gather_steps(pack, view, gsems)
    sbegin, sfinish = swap_steps(
        "lang", [(lambda t: outgoing.at[t], lambda m: arrived.at[m])], send, recv
    )
    own = [
        pltpu.make_async_copy(pack, view(s, None), own_sem.at[0]),
        pltpu.make_async_copy(outgoing.at[me], arrived.at[me], own_sem.at[1]),
    ]
    greet([("lang", everyone("lang")), ("seq", zpeers + [up, down])])
    sbegin()
    gbegin()
    for copy in own:
        copy.start()
    grest()
    sfinish()
    gfinish()
    for copy in own:
        copy.wait()


def return_kernel(results, returned, send, recv, own_sem):
    me = lax.axis_index("lang")
    begin, finish = swap_steps(
        "lang", [(lambda t: results.at[t], lambda m: returned.at[m])], send, recv
    )
    own = pltpu.make_async_copy(results.at[me], returned.at[me], own_sem.at[0])
    greet([("lang", everyone("lang"))])
    begin()
    own.start()
    finish()
    own.wait()


def prompt_kernel(mixed, q, k, v, g, rows, qh, kh, vh, gh, send, recv, own_sem, *gsems):
    s = lax.axis_index("seq")
    part = q.shape[1]
    count = mixed.shape[0]

    def view(shard, half):
        if half is None:
            return rows.at[pl.ds(pl.multiple_of(shard * count, count), count), :]
        size = count // 2
        return rows.at[pl.ds(pl.multiple_of(shard * count + half * size, size), size), :]

    def source(array):
        return lambda t: array.at[:, :, pl.ds(pl.multiple_of(t * HD, HD), HD)]

    def landing(array):
        return lambda m: array.at[:, pl.ds(pl.multiple_of(m * part, part), part), :]

    pieces = [(source(a), landing(b)) for a, b in ((q, qh), (k, kh), (v, vh), (g, gh))]
    gbegin, grest, gfinish = gather_steps(mixed, view, gsems)
    sbegin, sfinish = swap_steps("seq", pieces, send, recv)
    own = [pltpu.make_async_copy(mixed, view(s, None), own_sem.at[len(pieces)])]
    for i, (a, b) in enumerate(pieces):
        own.append(pltpu.make_async_copy(a(s), b(s), own_sem.at[i]))
    greet([("seq", everyone("seq"))])
    gbegin()
    sbegin()
    for copy in own:
        copy.start()
    grest()
    sfinish()
    gfinish()
    for copy in own:
        copy.wait()


def back_kernel(
    att, qg, kg, vg, partial, att_rows, latent, total, parts, mine, pair, done,
    send, recv, own_sem, rsend, rrecv, psend, precv, asend, arecv,
):
    s = lax.axis_index("seq")
    l = lax.axis_index("lang")
    group = lax.axis_size("lang") // 2
    high, j = lax.div(l, group), lax.rem(l, group)
    part = att_rows.shape[1]
    chunk = partial.shape[0] // group

    def source(array):
        return lambda t: array.at[:, pl.ds(pl.multiple_of(t * part, part), part), :]

    def landing(array):
        return lambda m: array.at[:, :, pl.ds(pl.multiple_of(m * HD, HD), HD)]

    pieces = [
        (source(att), landing(att_rows)),
        (source(qg), landing(latent.at[0])),
        (source(kg), landing(latent.at[1])),
        (source(vg), landing(latent.at[2])),
    ]
    sbegin, sfinish = swap_steps("seq", pieces, send, recv)
    own = [
        pltpu.make_async_copy(a(s), b(s), own_sem.at[i]) for i, (a, b) in enumerate(pieces)
    ]
    greet([("seq", everyone("seq")), ("lang", everyone("lang"))])

    def mate(k):
        return high * group + lax.rem(j + k, group)

    def piece(array, t):
        return array.at[pl.ds(pl.multiple_of(t * chunk, chunk), chunk), :]

    def scatter(k):
        t = lax.rem(j + k, group)
        return push(
            piece(partial, t), parts.at[group - k], rsend.at[k], rrecv.at[k], "lang", mate(k)
        )

    def spread(k):
        return push(done, piece(total, j), asend.at[k], arecv.at[k], "lang", mate(k))

    for k in range(1, group):
        scatter(k).start()
    sbegin()
    for copy in own:
        copy.start()
    keep = pltpu.make_async_copy(piece(partial, j), parts.at[0], own_sem.at[len(pieces)])
    keep.start()
    keep.wait()
    for k in range(1, group):
        scatter(k).wait()
    acc = parts[0].astype(F32)
    for k in range(1, group):
        acc = acc + parts[k].astype(F32)
    mine[...] = acc.astype(BF)
    other = lax.rem(l + group, 2 * group)
    cross = push(mine, pair, psend.at[0], precv.at[0], "lang", other)
    cross.start()
    cross.wait()
    done[...] = (mine[...].astype(F32) + pair[...].astype(F32)).astype(BF)
    for k in range(1, group):
        spread(k).start()
    last = pltpu.make_async_copy(done, piece(total, j), own_sem.at[len(pieces)])
    last.start()
    sfinish()
    for copy in own:
        copy.wait()
    last.wait()
    for k in range(1, group):
        spread(k).wait_send()
        t = lax.rem(j + group - k, group)
        push(done, piece(total, t), asend.at[k], arecv.at[k], "lang", mate(k)).wait_recv()


def attention_kernel(
    lengths, q_ref, g_ref, kl_ref, vl_ref, kp_ref, vp_ref,
    att_ref, qg_ref, kg_ref, vg_ref, pg_ref,
    kt, vt, kacc, vacc, e_s, d_s,
):
    page, block = pl.program_id(0), pl.program_id(1)
    length = lengths[page]
    lat = kl_ref.shape[1]
    keys_all = 2 * lat
    step = 256
    bq = q_ref.shape[1]
    scale = 1.0 / math.sqrt(HD)
    to_two = scale * math.log2(math.e)

    def key_part(i):
        at = i * step
        return kl_ref[0, pl.ds(at, step), :] if at < lat else kp_ref[pl.ds(at - lat, step), :]

    def value_part(i):
        at = i * step
        return vl_ref[0, pl.ds(at, step), :] if at < lat else vp_ref[pl.ds(at - lat, step), :]

    steps = keys_all // step

    @pl.when(block == 0)
    def _():
        for i in range(steps):
            kt[:, pl.ds(i * step, step)] = key_part(i).T
            vt[:, pl.ds(i * step, step)] = value_part(i).T
        kacc[...] = jnp.zeros_like(kacc)
        vacc[...] = jnp.zeros_like(vacc)

    q, g = q_ref[0], g_ref[0]
    nt = (((1,), (1,)), ((), ()))
    highest = jnp.full((1, bq), -jnp.inf, F32)
    for i in range(steps):
        scores = lax.dot_general(key_part(i), q, nt, preferred_element_type=F32)
        if i * step >= lat:
            at = i * step - lat + lax.broadcasted_iota(jnp.int32, (step, bq), 0)
            scores = jnp.where(at < length, scores, -jnp.inf)
        highest = jnp.maximum(highest, jnp.max(scores, axis=0, keepdims=True))
        e_s[pl.ds(i * step, step), :] = scores
    top = highest * to_two
    total = jnp.zeros((1, bq), F32)
    weighted = jnp.zeros((1, bq), F32)
    for i in range(steps):
        raised = jnp.exp2(e_s[pl.ds(i * step, step), :] * to_two - top)
        prob_grad = lax.dot_general(value_part(i), g, nt, preferred_element_type=F32)
        total = total + jnp.sum(raised, axis=0, keepdims=True)
        weighted = weighted + jnp.sum(raised * prob_grad, axis=0, keepdims=True)
        e_s[pl.ds(i * step, step), :] = raised
        d_s[pl.ds(i * step, step), :] = prob_grad
    inverse = 1.0 / total
    centre = weighted * inverse
    scaled = inverse * scale
    att_t = jnp.zeros((HD, bq), F32)
    qg_t = jnp.zeros((HD, bq), F32)
    for i in range(steps):
        at = pl.ds(i * step, step)
        raised = e_s[at, :]
        soft_low = (raised * inverse).astype(BF)
        score_grad = (raised * scaled * (d_s[at, :] - centre)).astype(BF)
        att_t = att_t + jnp.dot(vt[:, at], soft_low, preferred_element_type=F32)
        qg_t = qg_t + jnp.dot(kt[:, at], score_grad, preferred_element_type=F32)
        vacc[at, :] += jnp.dot(soft_low, g, preferred_element_type=F32)
        kacc[at, :] += jnp.dot(score_grad, q, preferred_element_type=F32)
    att_ref[0] = att_t.T.astype(BF)
    qg_ref[0] = qg_t.T.astype(BF)

    @pl.when(block == pl.num_programs(1) - 1)
    def _():
        kg_ref[0] = kacc[pl.ds(0, lat), :].astype(BF)
        vg_ref[0] = vacc[pl.ds(0, lat), :].astype(BF)
        pg_ref[:, pl.ds(0, HD)] = kacc[pl.ds(lat, lat), :].astype(BF)
        pg_ref[:, pl.ds(HD, HD)] = vacc[pl.ds(lat, lat), :].astype(BF)


def attention(lengths, q, g, k, v, kv):
    pages, lat, _ = q.shape
    bq = 256
    row = pl.BlockSpec((1, bq, HD), lambda p, b, _: (p, b, 0))
    full = pl.BlockSpec((1, lat, HD), lambda p, b, _: (p, 0, 0))
    key = pl.BlockSpec((lat, HD), lambda p, b, _: (p, 0))
    value = pl.BlockSpec((lat, HD), lambda p, b, _: (p, 1))
    both = pl.BlockSpec((lat, 2 * HD), lambda p, b, _: (p, 0))
    shape = jax.ShapeDtypeStruct((pages, lat, HD), BF)
    return pl.pallas_call(
        attention_kernel,
        grid_spec=pltpu.PrefetchScalarGridSpec(
            num_scalar_prefetch=1,
            grid=(pages, lat // bq),
            in_specs=[row, row, full, full, key, value],
            out_specs=[row, row, full, full, both],
            scratch_shapes=[
                pltpu.VMEM((HD, 2 * lat), BF),
                pltpu.VMEM((HD, 2 * lat), BF),
                pltpu.VMEM((2 * lat, HD), F32),
                pltpu.VMEM((2 * lat, HD), F32),
                pltpu.VMEM((2 * lat, bq), F32),
                pltpu.VMEM((2 * lat, bq), F32),
            ],
        ),
        out_shape=[shape] * 4 + [jax.ShapeDtypeStruct((pages * lat, 2 * HD), BF)],
        compiler_params=pltpu.CompilerParams(vmem_limit_bytes=48 << 20),
    )(lengths, q, g, k, v, kv, kv)


def remote(body, number, out_shape, scratch, *operands, vmem_outs=()):
    return pl.pallas_call(
        body,
        out_shape=out_shape,
        in_specs=[ANY] * len(operands),
        out_specs=[ANY] * len(out_shape),
        scratch_shapes=scratch,
        compiler_params=pltpu.CompilerParams(
            collective_id=number, has_side_effects=True, vmem_limit_bytes=32 << 20
        ),
    )(*operands)


def local(
    prompt_rows,
    expert_ids,
    expert_gates,
    w_gate,
    w_up,
    w_down,
    w_kv,
    prompt_lengths,
    latent_q,
    latent_k,
    latent_v,
    grad_out,
):
    lang_count = lax.axis_size("lang")
    seq_count = lax.axis_size("seq")
    experts_all = lang_count
    rows_local, model_width = prompt_rows.shape
    ff = w_gate.shape[2]
    capacity = 3 * rows_local // experts_all
    sds = jax.ShapeDtypeStruct
    targets = slot_targets(expert_ids, experts_all, capacity)
    slot_ids = jnp.arange(experts_all * capacity, dtype=jnp.int32)
    dispatch_mask = jnp.any(slot_ids[:, None, None] == targets[None, :, :], axis=2).astype(BF)
    outgoing = jnp.dot(dispatch_mask, prompt_rows, preferred_element_type=F32).astype(BF)
    outgoing = outgoing.reshape(experts_all, capacity, model_width)
    pack = jnp.concatenate([w_gate[0].T, w_up[0].T, w_down[0]], axis=0)
    whole, arrived = remote(
        dispatch_kernel,
        1,
        [sds((3 * ff, model_width), BF), sds(outgoing.shape, BF)],
        [DMA((1, lang_count)), DMA((1, lang_count)), DMA((2,))] + GATHER_SEMS,
        pack,
        outgoing,
    )
    tokens = arrived.reshape(experts_all * capacity, model_width)
    nt = (((1,), (1,)), ((), ()))
    gate_up = lax.dot_general(tokens, whole[: 2 * ff], nt, preferred_element_type=F32)
    hidden = (jax.nn.silu(gate_up[:, :ff]) * gate_up[:, ff:]).astype(BF)
    results = jnp.dot(hidden, whole[2 * ff :], preferred_element_type=F32).astype(BF)
    (returned,) = remote(
        return_kernel,
        2,
        [sds(outgoing.shape, BF)],
        [DMA((1, lang_count)), DMA((1, lang_count)), DMA((1,))],
        results.reshape(outgoing.shape),
    )
    returned = returned.reshape(experts_all * capacity, model_width)
    mixed_sum = jnp.zeros((rows_local, model_width), F32)
    for which in range(targets.shape[1]):
        picker = (targets[:, which][:, None] == slot_ids[None, :]).astype(BF)
        picked = jnp.dot(picker, returned, preferred_element_type=F32)
        mixed_sum = mixed_sum + expert_gates[:, which][:, None] * picked
    mixed = mixed_sum.astype(BF)
    pages, part, _ = latent_q.shape
    lat = part * seq_count
    heads = sds((pages, lat, HD), BF)
    group_rows, qh, kh, vh, gh = remote(
        prompt_kernel,
        3,
        [sds((rows_local * seq_count, model_width), BF)] + [heads] * 4,
        [DMA((4, seq_count)), DMA((4, seq_count)), DMA((5,))] + GATHER_SEMS,
        mixed,
        latent_q,
        latent_k,
        latent_v,
        grad_out,
    )
    kv = jnp.dot(
        group_rows, w_kv.reshape(model_width, 2 * HD), preferred_element_type=F32
    ).astype(BF)
    att, qg, kg, vg, prompt_grad = attention(prompt_lengths, qh, gh, kh, vh, kv)
    partial = lax.dot_general(
        group_rows, prompt_grad, (((0,), (0,)), ((), ())), preferred_element_type=F32
    ).astype(BF)
    half = lang_count // 2
    chunk = model_width // half
    att_rows, latent, total = remote(
        back_kernel,
        4,
        [
            sds(latent_q.shape, BF),
            sds((3,) + latent_q.shape, BF),
            sds(partial.shape, BF),
        ],
        [
            pltpu.VMEM((half, chunk, 2 * HD), BF),
            pltpu.VMEM((chunk, 2 * HD), BF),
            pltpu.VMEM((chunk, 2 * HD), BF),
            pltpu.VMEM((chunk, 2 * HD), BF),
            DMA((4, seq_count)),
            DMA((4, seq_count)),
            DMA((5,)),
            DMA((half,)),
            DMA((half,)),
            DMA((1,)),
            DMA((1,)),
            DMA((half,)),
            DMA((half,)),
        ],
        att,
        qg,
        kg,
        vg,
        partial,
    )
    grad_wkv = total.astype(F32).reshape(model_width, 2, HD)
    return (att_rows, latent, grad_wkv)


def solution(mesh):
    return jax.shard_map(
        local,
        mesh=mesh,
        in_specs=(
            P(("lang", "seq"), None),
            P(("lang", "seq"), None),
            P(("lang", "seq"), None),
            P("lang", "seq", None),
            P("lang", "seq", None),
            P("lang", None, "seq"),
            P(None, None, "seq"),
            P("lang"),
            P("lang", "seq", None),
            P("lang", "seq", None),
            P("lang", "seq", None),
            P("lang", "seq", None),
        ),
        out_specs=(P("lang", "seq", None), P(None, "lang", "seq", None), P(None, None, "seq")),
        check_vma=False,
    )
```

```python
import math

import jax
import jax.numpy as jnp
from jax import lax
from jax.experimental import pallas as pl
from jax.experimental.pallas import tpu as pltpu
from jax.sharding import PartitionSpec as P

HD = 128
MESH = pl.DeviceIdType.MESH
ANY = pl.BlockSpec(memory_space=pl.ANY)
BF = jnp.bfloat16
F32 = jnp.float32
DMA = pltpu.SemaphoreType.DMA
ZN = 4
CHUNKS = 2
YN = 4


def slot_targets(expert_ids, experts_all, capacity):
    rows_local, picks = expert_ids.shape
    flat_ids = expert_ids.reshape(rows_local * picks)
    expert_range = jnp.arange(experts_all, dtype=jnp.int32)
    onehot = (flat_ids[:, None] == expert_range[None, :]).astype(jnp.int32)
    earlier = jnp.cumsum(onehot, axis=0) - onehot
    slot_index = jnp.sum(earlier * onehot, axis=1)
    return (flat_ids * capacity + slot_index).reshape(rows_local, picks)


def push(src, dst, ssem, rsem, axis, target):
    return pltpu.make_async_remote_copy(
        src_ref=src,
        dst_ref=dst,
        send_sem=ssem,
        recv_sem=rsem,
        device_id={axis: target},
        device_id_type=MESH,
    )


def greet(axes):
    pl.semaphore_wait(pltpu.get_barrier_semaphore(), greet_all(axes))


def greet_all(axes):
    barrier = pltpu.get_barrier_semaphore()
    total = 0
    for axis in axes:
        count, of = everyone(axis)()

        def one(j, carry):
            pl.semaphore_signal(barrier, inc=1, device_id={axis: of(j)}, device_id_type=MESH)
            return carry

        lax.fori_loop(1, count, one, 0)
        total += count - 1
    return total


def everyone(axis):
    def make():
        n = lax.axis_size(axis)
        me = lax.axis_index(axis)
        return n, lambda j: lax.rem(me + j, n)

    return make


def ring_places():
    s = lax.axis_index("seq")
    y, z = lax.div(s, ZN), lax.rem(s, ZN)
    up = lax.rem(y + 1, YN) * ZN + z
    down = lax.rem(y + YN - 1, YN) * ZN + z
    return s, y, z, up, down


def gather_sems(chunks):
    return [DMA((chunks, ZN))] * 11


def gather_steps(source, view, sems):
    zl, zr, zin, us, ur, ds, dr, fus, fur, fds, fdr = sems
    s, y, z, up, down = ring_places()
    low_y = lax.rem(y + YN - 1, YN)
    high_y = lax.rem(y + 1, YN)

    def along(c, col, to_right, own):
        shard = y * ZN + col
        return push(
            source(c) if own else view(c, shard, None),
            view(c, shard, None),
            (zr if to_right else zl).at[c, col],
            zin.at[c, col],
            "seq",
            s + 1 if to_right else s - 1,
        )

    def across(c, col, own):
        shard = y * ZN + col
        src = source(c) if own else view(c, shard, None)
        dst = view(c, shard, None)
        return (
            push(src, dst, us.at[c, col], ur.at[c, col], "seq", up),
            push(src, dst, ds.at[c, col], dr.at[c, col], "seq", down),
        )

    def forwards(c, col):
        low = view(c, low_y * ZN + col, 0)
        high = view(c, high_y * ZN + col, 1)
        return (
            push(low, low, fus.at[c, col], fur.at[c, col], "seq", up),
            push(high, high, fds.at[c, col], fdr.at[c, col], "seq", down),
        )

    def pass_on(c, col):
        go_up, go_down = across(c, col, False)
        first, second = forwards(c, col)
        go_up.wait_recv()
        first.start()
        go_down.wait_recv()
        second.start()

    def each_side(t, do):
        @pl.when(z >= t)
        def _():
            do(z - t, True)

        @pl.when(z + t <= ZN - 1)
        def _():
            do(z + t, False)

    def on_way(to_right, do):
        @pl.when(z < ZN - 1 if to_right else z > 0)
        def _():
            do()

    def begin(c):
        for to_right in (True, False):
            on_way(to_right, lambda: along(c, z, to_right, True).start())
        for copy in across(c, z, True):
            copy.start()

    def step(c, t):
        def arrive(col, to_right):
            along(c, col, to_right, False).wait_recv()
            on_way(to_right, lambda: along(c, col, to_right, False).start())
            for copy in across(c, col, False):
                copy.start()

        each_side(t, arrive)

    def relay(c, t):
        if t == 0:
            pass_on(c, z)
        else:
            each_side(t, lambda col, to_right: pass_on(c, col))

    def finish(c):
        for to_right in (True, False):
            on_way(to_right, lambda: along(c, z, to_right, True).wait_send())
        for copy in across(c, z, True):
            copy.wait_send()
        for copy in forwards(c, z):
            copy.wait()
        for t in range(1, ZN):

            def ended(col, to_right):
                on_way(to_right, lambda: along(c, col, to_right, False).wait_send())
                for copy in across(c, col, False):
                    copy.wait_send()
                for copy in forwards(c, col):
                    copy.wait()

            each_side(t, ended)

    return begin, step, relay, finish


def swap_steps(axis, pieces, send, recv):
    n = lax.axis_size(axis)
    me = lax.axis_index(axis)

    def copy(i, j):
        target = lax.rem(me + j, n)
        source, landing = pieces[i]
        return push(source(target), landing(me), send.at[i, j], recv.at[i, j], axis, target)

    def begin():
        def one(j, carry):
            for i in range(len(pieces)):
                copy(i, j).start()
            return carry

        lax.fori_loop(1, n, one, 0)

    def finish():
        def one(j, carry):
            for i in range(len(pieces)):
                copy(i, j).wait()
            return carry

        lax.fori_loop(1, n, one, 0)

    return begin, finish


def latent_pieces(pairs):
    part = pairs[0][0].shape[1]

    def source(array):
        return lambda t: array.at[:, :, pl.ds(pl.multiple_of(t * HD, HD), HD)]

    def landing(array):
        return lambda m: array.at[:, pl.ds(pl.multiple_of(m * part, part), part), :]

    return [(source(a), landing(b)) for a, b in pairs]


def dispatch_kernel(
    pack, outgoing, q, g, whole, arrived, qh, gh, send, recv, lsend, lrecv, own_sem, *gsems
):
    s = lax.axis_index("seq")
    pieces = latent_pieces([(q, qh), (g, gh)])
    lbegin, lfinish = swap_steps("seq", pieces, lsend, lrecv)
    me = lax.axis_index("lang")
    chunks = 3
    size = pack.shape[0] // chunks

    def view(c, shard, half):
        columns = pl.ds(pl.multiple_of(shard * HD, HD), HD)
        if half is None:
            return whole.at[pl.ds(c * size, size), columns]
        rows = size // 2
        return whole.at[pl.ds(c * size + half * rows, rows), columns]

    begin, step, relay, finish = gather_steps(
        lambda c: pack.at[pl.ds(c * size, size), :], view, gsems
    )
    sbegin, sfinish = swap_steps(
        "lang", [(lambda t: outgoing.at[t], lambda m: arrived.at[m])], send, recv
    )
    own = [
        pltpu.make_async_copy(
            pack, whole.at[:, pl.ds(pl.multiple_of(s * HD, HD), HD)], own_sem.at[0]
        ),
        pltpu.make_async_copy(outgoing.at[me], arrived.at[me], own_sem.at[1]),
    ]
    for i, (a, b) in enumerate(pieces):
        own.append(pltpu.make_async_copy(a(s), b(s), own_sem.at[i + 2]))
    greet(["lang", "seq"])
    for c in range(chunks):
        begin(c)
    sbegin()
    for copy in own:
        copy.start()
    for t in range(1, ZN):
        for c in range(chunks):
            step(c, t)
            relay(c, t - 1)
        if t == 1:
            lbegin()
    for c in range(chunks):
        relay(c, ZN - 1)
    sfinish()
    lfinish()
    for c in range(chunks):
        finish(c)
    for copy in own:
        copy.wait()


def prompt_kernel(
    results, pick, gates, k, v, rows, kh, vh,
    returned, mixed, rsend, rrecv, send, recv, own_sem, *gsems,
):
    s = lax.axis_index("seq")
    me = lax.axis_index("lang")
    count, width = mixed.shape
    chunks = rsend.shape[0]
    wide = width // chunks

    def view(c, shard, half):
        columns = pl.ds(c * wide, wide)
        if half is None:
            return rows.at[pl.ds(pl.multiple_of(shard * count, count), count), columns]
        size = count // 2
        at = pl.multiple_of(shard * count + half * size, size)
        return rows.at[pl.ds(at, size), columns]

    pieces = latent_pieces([(k, kh), (v, vh)])
    begin, step, relay, finish = gather_steps(
        lambda c: mixed.at[:, pl.ds(c * wide, wide)], view, gsems
    )
    swaps = [
        swap_steps("seq", [pieces[i]], send.at[pl.ds(i, 1)], recv.at[pl.ds(i, 1)])
        for i in range(2)
    ]

    def back(c):
        columns = pl.ds(c * wide, wide)
        return swap_steps(
            "lang",
            [(lambda t: results.at[t, :, columns], lambda m: returned.at[m, :, columns])],
            rsend.at[pl.ds(c, 1)],
            rrecv.at[pl.ds(c, 1)],
        )

    backs = [back(c) for c in range(chunks)]
    own = [pltpu.make_async_copy(results.at[me], returned.at[me], own_sem.at[0])]
    for i, (a, b) in enumerate(pieces):
        own.append(pltpu.make_async_copy(a(s), b(s), own_sem.at[i + 1]))
    greet(["seq", "lang"])
    for copy in own:
        copy.start()
    for c in range(chunks):
        backs[c][0]()
    own[0].wait()
    places = []

    def mix(c):
        backs[c][1]()
        columns = pl.ds(c * wide, wide)
        slots = returned[:, :, columns].astype(F32)
        slots = slots.reshape(slots.shape[0] * slots.shape[1], wide).astype(BF)
        total = jnp.zeros((count, wide), F32)
        for which in range(pick.shape[0]):
            picked = jnp.dot(pick[which], slots, preferred_element_type=F32)
            total = total + gates[:, which : which + 1] * picked
        mixed[:, columns] = total.astype(BF)
        place = pltpu.make_async_copy(
            mixed.at[:, columns], view(c, s, None), own_sem.at[3 + c]
        )
        place.start()
        places.append(place)
        begin(c)

    mix(0)
    swaps[0][0]()
    step(0, 1)
    mix(1)
    relay(0, 0)
    step(0, 2)
    step(1, 1)
    swaps[1][0]()
    relay(0, 1)
    relay(1, 0)
    step(0, 3)
    step(1, 2)
    relay(0, 2)
    relay(1, 1)
    step(1, 3)
    relay(0, 3)
    relay(1, 2)
    relay(1, 3)
    for swap in swaps:
        swap[1]()
    for c in range(chunks):
        finish(c)
    for copy in own[1:] + places:
        copy.wait()


def back_kernel(
    att, qg, kg, vg, partial, att_rows, latent, total, parts, mine, pair, done,
    send, recv, own_sem, rsend, rrecv, psend, precv, asend, arecv,
):
    s = lax.axis_index("seq")
    l = lax.axis_index("lang")
    group = lax.axis_size("lang") // 2
    high, j = lax.div(l, group), lax.rem(l, group)
    part = att_rows.shape[1]
    chunk = partial.shape[0] // group

    def source(array):
        return lambda t: array.at[:, pl.ds(pl.multiple_of(t * part, part), part), :]

    def landing(array):
        return lambda m: array.at[:, :, pl.ds(pl.multiple_of(m * HD, HD), HD)]

    pieces = [
        (source(att), landing(att_rows)),
        (source(qg), landing(latent.at[0])),
        (source(kg), landing(latent.at[1])),
        (source(vg), landing(latent.at[2])),
    ]
    sbegin, sfinish = swap_steps("seq", pieces, send, recv)
    own = [
        pltpu.make_async_copy(a(s), b(s), own_sem.at[i]) for i, (a, b) in enumerate(pieces)
    ]
    greet(["seq", "lang"])

    def mate(k):
        return high * group + lax.rem(j + k, group)

    def piece(array, t):
        return array.at[pl.ds(pl.multiple_of(t * chunk, chunk), chunk), :]

    def scatter(k):
        t = lax.rem(j + k, group)
        return push(
            piece(partial, t), parts.at[group - k], rsend.at[k], rrecv.at[k], "lang", mate(k)
        )

    def spread(k):
        return push(done, piece(total, j), asend.at[k], arecv.at[k], "lang", mate(k))

    for k in range(1, group):
        scatter(k).start()
    sbegin()
    for copy in own:
        copy.start()
    keep = pltpu.make_async_copy(piece(partial, j), parts.at[0], own_sem.at[len(pieces)])
    keep.start()
    keep.wait()
    for k in range(1, group):
        scatter(k).wait()
    acc = parts[0].astype(F32)
    for k in range(1, group):
        acc = acc + parts[k].astype(F32)
    mine[...] = acc.astype(BF)
    other = lax.rem(l + group, 2 * group)
    cross = push(mine, pair, psend.at[0], precv.at[0], "lang", other)
    cross.start()
    cross.wait()
    done[...] = (mine[...].astype(F32) + pair[...].astype(F32)).astype(BF)
    for k in range(1, group):
        spread(k).start()
    last = pltpu.make_async_copy(done, piece(total, j), own_sem.at[len(pieces)])
    last.start()
    sfinish()
    for copy in own:
        copy.wait()
    last.wait()
    for k in range(1, group):
        spread(k).wait_send()
        t = lax.rem(j + group - k, group)
        push(done, piece(total, t), asend.at[k], arecv.at[k], "lang", mate(k)).wait_recv()


def attention_kernel(
    lengths, q_ref, g_ref, kl_ref, vl_ref, kp_ref, vp_ref,
    att_ref, qg_ref, kg_ref, vg_ref, pg_ref,
    kt, vt, kacc, vacc, e_s, d_s,
):
    page, block = pl.program_id(0), pl.program_id(1)
    length = lengths[page]
    lat = kl_ref.shape[1]
    keys_all = 2 * lat
    step = 256
    bq = q_ref.shape[1]
    scale = 1.0 / math.sqrt(HD)
    to_two = scale * math.log2(math.e)

    def key_part(i):
        at = i * step
        return kl_ref[0, pl.ds(at, step), :] if at < lat else kp_ref[pl.ds(at - lat, step), :]

    def value_part(i):
        at = i * step
        return vl_ref[0, pl.ds(at, step), :] if at < lat else vp_ref[pl.ds(at - lat, step), :]

    steps = keys_all // step

    @pl.when(block == 0)
    def _():
        for i in range(steps):
            kt[:, pl.ds(i * step, step)] = key_part(i).T
            vt[:, pl.ds(i * step, step)] = value_part(i).T
        kacc[...] = jnp.zeros_like(kacc)
        vacc[...] = jnp.zeros_like(vacc)

    q, g = q_ref[0], g_ref[0]
    nt = (((1,), (1,)), ((), ()))
    highest = jnp.full((1, bq), -jnp.inf, F32)
    for i in range(steps):
        scores = lax.dot_general(key_part(i), q, nt, preferred_element_type=F32)
        if i * step >= lat:
            at = i * step - lat + lax.broadcasted_iota(jnp.int32, (step, bq), 0)
            scores = jnp.where(at < length, scores, -jnp.inf)
        highest = jnp.maximum(highest, jnp.max(scores, axis=0, keepdims=True))
        e_s[pl.ds(i * step, step), :] = scores
    top = highest * to_two
    total = jnp.zeros((1, bq), F32)
    weighted = jnp.zeros((1, bq), F32)
    for i in range(steps):
        raised = jnp.exp2(e_s[pl.ds(i * step, step), :] * to_two - top)
        prob_grad = lax.dot_general(value_part(i), g, nt, preferred_element_type=F32)
        total = total + jnp.sum(raised, axis=0, keepdims=True)
        weighted = weighted + jnp.sum(raised * prob_grad, axis=0, keepdims=True)
        e_s[pl.ds(i * step, step), :] = raised
        d_s[pl.ds(i * step, step), :] = prob_grad
    inverse = 1.0 / total
    centre = weighted * inverse
    scaled = inverse * scale
    att_t = jnp.zeros((HD, bq), F32)
    qg_t = jnp.zeros((HD, bq), F32)
    for i in range(steps):
        at = pl.ds(i * step, step)
        raised = e_s[at, :]
        soft_low = (raised * inverse).astype(BF)
        score_grad = (raised * scaled * (d_s[at, :] - centre)).astype(BF)
        att_t = att_t + jnp.dot(vt[:, at], soft_low, preferred_element_type=F32)
        qg_t = qg_t + jnp.dot(kt[:, at], score_grad, preferred_element_type=F32)
        vacc[at, :] += jnp.dot(soft_low, g, preferred_element_type=F32)
        kacc[at, :] += jnp.dot(score_grad, q, preferred_element_type=F32)
    att_ref[0] = att_t.T.astype(BF)
    qg_ref[0] = qg_t.T.astype(BF)

    @pl.when(block == pl.num_programs(1) - 1)
    def _():
        kg_ref[0] = kacc[pl.ds(0, lat), :].astype(BF)
        vg_ref[0] = vacc[pl.ds(0, lat), :].astype(BF)
        pg_ref[:, pl.ds(0, HD)] = kacc[pl.ds(lat, lat), :].astype(BF)
        pg_ref[:, pl.ds(HD, HD)] = vacc[pl.ds(lat, lat), :].astype(BF)


def attention(lengths, q, g, k, v, kv):
    pages, lat, _ = q.shape
    bq = 256
    row = pl.BlockSpec((1, bq, HD), lambda p, b, _: (p, b, 0))
    full = pl.BlockSpec((1, lat, HD), lambda p, b, _: (p, 0, 0))
    key = pl.BlockSpec((lat, HD), lambda p, b, _: (p, 0))
    value = pl.BlockSpec((lat, HD), lambda p, b, _: (p, 1))
    both = pl.BlockSpec((lat, 2 * HD), lambda p, b, _: (p, 0))
    shape = jax.ShapeDtypeStruct((pages, lat, HD), BF)
    return pl.pallas_call(
        attention_kernel,
        grid_spec=pltpu.PrefetchScalarGridSpec(
            num_scalar_prefetch=1,
            grid=(pages, lat // bq),
            in_specs=[row, row, full, full, key, value],
            out_specs=[row, row, full, full, both],
            scratch_shapes=[
                pltpu.VMEM((HD, 2 * lat), BF),
                pltpu.VMEM((HD, 2 * lat), BF),
                pltpu.VMEM((2 * lat, HD), F32),
                pltpu.VMEM((2 * lat, HD), F32),
                pltpu.VMEM((2 * lat, bq), F32),
                pltpu.VMEM((2 * lat, bq), F32),
            ],
        ),
        out_shape=[shape] * 4 + [jax.ShapeDtypeStruct((pages * lat, 2 * HD), BF)],
        compiler_params=pltpu.CompilerParams(vmem_limit_bytes=48 << 20),
    )(lengths, q, g, k, v, kv, kv)


def remote(body, number, out_shape, scratch, *operands, in_vmem=()):
    return pl.pallas_call(
        body,
        out_shape=out_shape,
        in_specs=[
            pl.BlockSpec(memory_space=pltpu.VMEM) if i in in_vmem else ANY
            for i in range(len(operands))
        ],
        out_specs=[ANY] * len(out_shape),
        scratch_shapes=scratch,
        compiler_params=pltpu.CompilerParams(
            collective_id=number, has_side_effects=True, vmem_limit_bytes=32 << 20
        ),
    )(*operands)


def local(
    prompt_rows,
    expert_ids,
    expert_gates,
    w_gate,
    w_up,
    w_down,
    w_kv,
    prompt_lengths,
    latent_q,
    latent_k,
    latent_v,
    grad_out,
):
    lang_count = lax.axis_size("lang")
    seq_count = lax.axis_size("seq")
    experts_all = lang_count
    rows_local, model_width = prompt_rows.shape
    ff = w_gate.shape[2]
    capacity = 3 * rows_local // experts_all
    sds = jax.ShapeDtypeStruct
    targets = slot_targets(expert_ids, experts_all, capacity)
    slot_ids = jnp.arange(experts_all * capacity, dtype=jnp.int32)
    dispatch_mask = jnp.any(slot_ids[:, None, None] == targets[None, :, :], axis=2).astype(BF)
    outgoing = jnp.dot(dispatch_mask, prompt_rows, preferred_element_type=F32).astype(BF)
    outgoing = outgoing.reshape(experts_all, capacity, model_width)
    pack = jnp.concatenate([w_gate[0].T, w_up[0].T, w_down[0]], axis=0)
    pages, part, _ = latent_q.shape
    lat = part * seq_count
    heads = sds((pages, lat, HD), BF)
    whole, arrived, qh, gh = remote(
        dispatch_kernel,
        1,
        [sds((3 * ff, model_width), BF), sds(outgoing.shape, BF), heads, heads],
        [
            DMA((1, lang_count)),
            DMA((1, lang_count)),
            DMA((2, seq_count)),
            DMA((2, seq_count)),
            DMA((4,)),
        ]
        + gather_sems(3),
        pack,
        outgoing,
        latent_q,
        grad_out,
    )
    tokens = arrived.reshape(experts_all * capacity, model_width)
    nt = (((1,), (1,)), ((), ()))
    gate_up = lax.dot_general(tokens, whole[: 2 * ff], nt, preferred_element_type=F32)
    hidden = (jax.nn.silu(gate_up[:, :ff]) * gate_up[:, ff:]).astype(BF)
    results = jnp.dot(hidden, whole[2 * ff :], preferred_element_type=F32).astype(BF)
    pick = (targets.T[:, :, None] == slot_ids[None, None, :]).astype(BF)
    group_rows, kh, vh = remote(
        prompt_kernel,
        3,
        [sds((rows_local * seq_count, model_width), BF)] + [heads] * 2,
        [
            pltpu.VMEM(outgoing.shape, BF),
            pltpu.VMEM((rows_local, model_width), BF),
            DMA((CHUNKS, lang_count)),
            DMA((CHUNKS, lang_count)),
            DMA((2, seq_count)),
            DMA((2, seq_count)),
            DMA((3 + CHUNKS,)),
        ]
        + gather_sems(CHUNKS),
        results.reshape(outgoing.shape),
        pick,
        expert_gates,
        latent_k,
        latent_v,
        in_vmem=(1, 2),
    )
    kv = jnp.dot(
        group_rows, w_kv.reshape(model_width, 2 * HD), preferred_element_type=F32
    ).astype(BF)
    att, qg, kg, vg, prompt_grad = attention(prompt_lengths, qh, gh, kh, vh, kv)
    partial = lax.dot_general(
        group_rows, prompt_grad, (((0,), (0,)), ((), ())), preferred_element_type=F32
    ).astype(BF)
    half = lang_count // 2
    chunk = model_width // half
    att_rows, latent, total = remote(
        back_kernel,
        4,
        [
            sds(latent_q.shape, BF),
            sds((3,) + latent_q.shape, BF),
            sds(partial.shape, BF),
        ],
        [
            pltpu.VMEM((half, chunk, 2 * HD), BF),
            pltpu.VMEM((chunk, 2 * HD), BF),
            pltpu.VMEM((chunk, 2 * HD), BF),
            pltpu.VMEM((chunk, 2 * HD), BF),
            DMA((4, seq_count)),
            DMA((4, seq_count)),
            DMA((5,)),
            DMA((half,)),
            DMA((half,)),
            DMA((1,)),
            DMA((1,)),
            DMA((half,)),
            DMA((half,)),
        ],
        att,
        qg,
        kg,
        vg,
        partial,
    )
    grad_wkv = total.astype(F32).reshape(model_width, 2, HD)
    return (att_rows, latent, grad_wkv)


def solution(mesh):
    return jax.shard_map(
        local,
        mesh=mesh,
        in_specs=(
            P(("lang", "seq"), None),
            P(("lang", "seq"), None),
            P(("lang", "seq"), None),
            P("lang", "seq", None),
            P("lang", "seq", None),
            P("lang", None, "seq"),
            P(None, None, "seq"),
            P("lang"),
            P("lang", "seq", None),
            P("lang", "seq", None),
            P("lang", "seq", None),
            P("lang", "seq", None),
        ),
        out_specs=(P("lang", "seq", None), P(None, "lang", "seq", None), P(None, None, "seq")),
        check_vma=False,
    )
```

```python
import math

import jax
import jax.numpy as jnp
from jax import lax
from jax.experimental import pallas as pl
from jax.experimental.pallas import tpu as pltpu
from jax.sharding import PartitionSpec as P

HD = 128
MESH = pl.DeviceIdType.MESH
ANY = pl.BlockSpec(memory_space=pl.ANY)
BF = jnp.bfloat16
F32 = jnp.float32
DMA = pltpu.SemaphoreType.DMA
ZN = 4
CHUNKS = 2
YN = 4


def slot_targets(expert_ids, experts_all, capacity):
    rows_local, picks = expert_ids.shape
    flat_ids = expert_ids.reshape(rows_local * picks)
    expert_range = jnp.arange(experts_all, dtype=jnp.int32)
    onehot = (flat_ids[:, None] == expert_range[None, :]).astype(jnp.int32)
    earlier = jnp.cumsum(onehot, axis=0) - onehot
    slot_index = jnp.sum(earlier * onehot, axis=1)
    return (flat_ids * capacity + slot_index).reshape(rows_local, picks)


def push(src, dst, ssem, rsem, axis, target):
    return pltpu.make_async_remote_copy(
        src_ref=src,
        dst_ref=dst,
        send_sem=ssem,
        recv_sem=rsem,
        device_id={axis: target},
        device_id_type=MESH,
    )


def greet(axes):
    pl.semaphore_wait(pltpu.get_barrier_semaphore(), greet_all(axes))


def greet_all(axes):
    barrier = pltpu.get_barrier_semaphore()
    total = 0
    for axis in axes:
        count, of = everyone(axis)()

        def one(j, carry):
            pl.semaphore_signal(barrier, inc=1, device_id={axis: of(j)}, device_id_type=MESH)
            return carry

        lax.fori_loop(1, count, one, 0)
        total += count - 1
    return total


def everyone(axis):
    def make():
        n = lax.axis_size(axis)
        me = lax.axis_index(axis)
        return n, lambda j: lax.rem(me + j, n)

    return make


def ring_places():
    s = lax.axis_index("seq")
    y, z = lax.div(s, ZN), lax.rem(s, ZN)
    up = lax.rem(y + 1, YN) * ZN + z
    down = lax.rem(y + YN - 1, YN) * ZN + z
    return s, y, z, up, down


def gather_sems(chunks):
    return [DMA((chunks, ZN))] * 11


def gather_steps(source, view, sems):
    zl, zr, zin, us, ur, ds, dr, fus, fur, fds, fdr = sems
    s, y, z, up, down = ring_places()
    low_y = lax.rem(y + YN - 1, YN)
    high_y = lax.rem(y + 1, YN)

    def along(c, col, to_right, own):
        shard = y * ZN + col
        return push(
            source(c) if own else view(c, shard, None),
            view(c, shard, None),
            (zr if to_right else zl).at[c, col],
            zin.at[c, col],
            "seq",
            s + 1 if to_right else s - 1,
        )

    def across(c, col, own):
        shard = y * ZN + col
        src = source(c) if own else view(c, shard, None)
        dst = view(c, shard, None)
        return (
            push(src, dst, us.at[c, col], ur.at[c, col], "seq", up),
            push(src, dst, ds.at[c, col], dr.at[c, col], "seq", down),
        )

    def forwards(c, col):
        low = view(c, low_y * ZN + col, 0)
        high = view(c, high_y * ZN + col, 1)
        return (
            push(low, low, fus.at[c, col], fur.at[c, col], "seq", up),
            push(high, high, fds.at[c, col], fdr.at[c, col], "seq", down),
        )

    def pass_on(c, col):
        go_up, go_down = across(c, col, False)
        first, second = forwards(c, col)
        go_up.wait_recv()
        first.start()
        go_down.wait_recv()
        second.start()

    def each_side(t, do):
        @pl.when(z >= t)
        def _():
            do(z - t, True)

        @pl.when(z + t <= ZN - 1)
        def _():
            do(z + t, False)

    def on_way(to_right, do):
        @pl.when(z < ZN - 1 if to_right else z > 0)
        def _():
            do()

    def begin(c):
        for to_right in (True, False):
            on_way(to_right, lambda: along(c, z, to_right, True).start())
        for copy in across(c, z, True):
            copy.start()

    def step(c, t):
        def arrive(col, to_right):
            along(c, col, to_right, False).wait_recv()
            on_way(to_right, lambda: along(c, col, to_right, False).start())
            for copy in across(c, col, False):
                copy.start()

        each_side(t, arrive)

    def relay(c, t):
        if t == 0:
            pass_on(c, z)
        else:
            each_side(t, lambda col, to_right: pass_on(c, col))

    def finish(c):
        for to_right in (True, False):
            on_way(to_right, lambda: along(c, z, to_right, True).wait_send())
        for copy in across(c, z, True):
            copy.wait_send()
        for copy in forwards(c, z):
            copy.wait()
        for t in range(1, ZN):

            def ended(col, to_right):
                on_way(to_right, lambda: along(c, col, to_right, False).wait_send())
                for copy in across(c, col, False):
                    copy.wait_send()
                for copy in forwards(c, col):
                    copy.wait()

            each_side(t, ended)

    return begin, step, relay, finish


def swap_steps(axis, pieces, send, recv):
    n = lax.axis_size(axis)
    me = lax.axis_index(axis)

    def copy(i, j):
        target = lax.rem(me + j, n)
        source, landing = pieces[i]
        return push(source(target), landing(me), send.at[i, j], recv.at[i, j], axis, target)

    def begin():
        def one(j, carry):
            for i in range(len(pieces)):
                copy(i, j).start()
            return carry

        lax.fori_loop(1, n, one, 0)

    def finish():
        def one(j, carry):
            for i in range(len(pieces)):
                copy(i, j).wait()
            return carry

        lax.fori_loop(1, n, one, 0)

    return begin, finish


def latent_pieces(pairs):
    part = pairs[0][0].shape[1]

    def source(array):
        return lambda t: array.at[:, :, pl.ds(pl.multiple_of(t * HD, HD), HD)]

    def landing(array):
        return lambda m: array.at[:, pl.ds(pl.multiple_of(m * part, part), part), :]

    return [(source(a), landing(b)) for a, b in pairs]


def dispatch_kernel(
    pack, outgoing, q, g, whole, arrived, qh, gh, send, recv, lsend, lrecv, own_sem, *gsems
):
    s = lax.axis_index("seq")
    pieces = latent_pieces([(q, qh), (g, gh)])
    lbegin, lfinish = swap_steps("seq", pieces, lsend, lrecv)
    me = lax.axis_index("lang")
    chunks = 3
    size = pack.shape[0] // chunks

    def view(c, shard, half):
        columns = pl.ds(pl.multiple_of(shard * HD, HD), HD)
        if half is None:
            return whole.at[pl.ds(c * size, size), columns]
        rows = size // 2
        return whole.at[pl.ds(c * size + half * rows, rows), columns]

    begin, step, relay, finish = gather_steps(
        lambda c: pack.at[pl.ds(c * size, size), :], view, gsems
    )
    sbegin, sfinish = swap_steps(
        "lang", [(lambda t: outgoing.at[t], lambda m: arrived.at[m])], send, recv
    )
    own = [
        pltpu.make_async_copy(
            pack, whole.at[:, pl.ds(pl.multiple_of(s * HD, HD), HD)], own_sem.at[0]
        ),
        pltpu.make_async_copy(outgoing.at[me], arrived.at[me], own_sem.at[1]),
    ]
    for i, (a, b) in enumerate(pieces):
        own.append(pltpu.make_async_copy(a(s), b(s), own_sem.at[i + 2]))
    greet(["lang", "seq"])
    for c in range(chunks):
        begin(c)
    sbegin()
    for copy in own:
        copy.start()
    for t in range(1, ZN):
        for c in range(chunks):
            step(c, t)
            relay(c, t - 1)
        if t == 1:
            lbegin()
    for c in range(chunks):
        relay(c, ZN - 1)
    sfinish()
    lfinish()
    for c in range(chunks):
        finish(c)
    for copy in own:
        copy.wait()


def prompt_kernel(
    results, pick, gates, k, v, rows, kh, vh,
    returned, mixed, rsend, rrecv, send, recv, own_sem, *gsems,
):
    s = lax.axis_index("seq")
    me = lax.axis_index("lang")
    count, width = mixed.shape
    chunks = rsend.shape[0]
    wide = width // chunks

    def view(c, shard, half):
        columns = pl.ds(c * wide, wide)
        if half is None:
            return rows.at[pl.ds(pl.multiple_of(shard * count, count), count), columns]
        size = count // 2
        at = pl.multiple_of(shard * count + half * size, size)
        return rows.at[pl.ds(at, size), columns]

    pieces = latent_pieces([(k, kh), (v, vh)])
    begin, step, relay, finish = gather_steps(
        lambda c: mixed.at[:, pl.ds(c * wide, wide)], view, gsems
    )
    swaps = [
        swap_steps("seq", [pieces[i]], send.at[pl.ds(i, 1)], recv.at[pl.ds(i, 1)])
        for i in range(2)
    ]

    def back(c):
        columns = pl.ds(c * wide, wide)
        return swap_steps(
            "lang",
            [(lambda t: results.at[t, :, columns], lambda m: returned.at[m, :, columns])],
            rsend.at[pl.ds(c, 1)],
            rrecv.at[pl.ds(c, 1)],
        )

    backs = [back(c) for c in range(chunks)]
    own = [pltpu.make_async_copy(results.at[me], returned.at[me], own_sem.at[0])]
    for i, (a, b) in enumerate(pieces):
        own.append(pltpu.make_async_copy(a(s), b(s), own_sem.at[i + 1]))
    greet(["seq", "lang"])
    for copy in own:
        copy.start()
    for c in range(chunks):
        backs[c][0]()
    own[0].wait()
    places = []

    def mix(c):
        backs[c][1]()
        columns = pl.ds(c * wide, wide)
        slots = returned[:, :, columns].astype(F32)
        slots = slots.reshape(slots.shape[0] * slots.shape[1], wide).astype(BF)
        total = jnp.zeros((count, wide), F32)
        for which in range(pick.shape[0]):
            picked = jnp.dot(pick[which], slots, preferred_element_type=F32)
            total = total + gates[:, which : which + 1] * picked
        mixed[:, columns] = total.astype(BF)
        place = pltpu.make_async_copy(
            mixed.at[:, columns], view(c, s, None), own_sem.at[3 + c]
        )
        place.start()
        places.append(place)
        begin(c)

    mix(0)
    swaps[0][0]()
    step(0, 1)
    mix(1)
    relay(0, 0)
    step(0, 2)
    step(1, 1)
    swaps[1][0]()
    relay(0, 1)
    relay(1, 0)
    step(0, 3)
    step(1, 2)
    relay(0, 2)
    relay(1, 1)
    step(1, 3)
    relay(0, 3)
    relay(1, 2)
    relay(1, 3)
    for swap in swaps:
        swap[1]()
    for c in range(chunks):
        finish(c)
    for copy in own[1:] + places:
        copy.wait()


def attend_kernel(
    lengths, q_ref, g_ref, k_ref, v_ref, kv_ref, rows_hbm, att_rows, latent, total,
    rows, att, qg, kg, vg, pg_t, kt, vt, kacc, vacc, e_s, d_s,
    outbound, parts, mine, pair, done,
    send, recv, own_sem, rsend, rrecv, psend, precv, asend, arecv,
):
    s = lax.axis_index("seq")
    l = lax.axis_index("lang")
    n = lax.axis_size("seq")
    y = lax.div(s, ZN)
    group = lax.axis_size("lang") // 2
    high, j = lax.div(l, group), lax.rem(l, group)
    pages, lat, _ = q_ref.shape
    part = att_rows.shape[1]
    chunk = rows.shape[1] // group
    sources = [att, qg, kg, vg]
    landings = [att_rows, latent.at[0], latent.at[1], latent.at[2]]
    fetch = pltpu.make_async_copy(rows_hbm, rows, own_sem.at[0])
    fetch.start()
    greet(["seq", "lang"])

    def out(i, page, to, frm):
        return push(
            sources[i].at[page, pl.ds(pl.multiple_of(to * part, part), part), :],
            landings[i].at[page, :, pl.ds(pl.multiple_of(frm * HD, HD), HD)],
            send.at[i, page, to],
            recv.at[i, page, frm],
            "seq",
            to,
        )

    step = 256
    blocks = YN
    bq = lat // blocks
    keys_all = 2 * lat
    steps = keys_all // step
    scale = 1.0 / math.sqrt(HD)
    to_two = scale * math.log2(math.e)
    nt = (((1,), (1,)), ((), ()))

    def one_block(turn, carry):
        page, at_block = lax.div(turn, blocks), lax.rem(turn, blocks)
        block = lax.rem(y + 1 + at_block, blocks)
        length = jnp.where(page == 0, lengths[0], lengths[1])

        def key_part(i):
            at = i * step
            if at < lat:
                return k_ref[page, pl.ds(at, step), :]
            return kv_ref[pl.ds(pl.multiple_of(page * lat + at - lat, step), step), pl.ds(0, HD)]

        def value_part(i):
            at = i * step
            if at < lat:
                return v_ref[page, pl.ds(at, step), :]
            return kv_ref[pl.ds(pl.multiple_of(page * lat + at - lat, step), step), pl.ds(HD, HD)]

        @pl.when(at_block == 0)
        def _():
            for i in range(steps):
                kt[:, pl.ds(i * step, step)] = key_part(i).T
                vt[:, pl.ds(i * step, step)] = value_part(i).T
            kacc[...] = jnp.zeros_like(kacc)
            vacc[...] = jnp.zeros_like(vacc)

        places = pl.ds(pl.multiple_of(block * bq, bq), bq)
        q, g = q_ref[page, places, :], g_ref[page, places, :]
        highest = jnp.full((1, bq), -jnp.inf, F32)
        for i in range(steps):
            scores = lax.dot_general(key_part(i), q, nt, preferred_element_type=F32)
            if i * step >= lat:
                at = i * step - lat + lax.broadcasted_iota(jnp.int32, (step, bq), 0)
                scores = jnp.where(at < length, scores, -jnp.inf)
            highest = jnp.maximum(highest, jnp.max(scores, axis=0, keepdims=True))
            e_s[pl.ds(i * step, step), :] = scores
        top = highest * to_two
        weight = jnp.zeros((1, bq), F32)
        weighted = jnp.zeros((1, bq), F32)
        for i in range(steps):
            raised = jnp.exp2(e_s[pl.ds(i * step, step), :] * to_two - top)
            prob_grad = lax.dot_general(value_part(i), g, nt, preferred_element_type=F32)
            weight = weight + jnp.sum(raised, axis=0, keepdims=True)
            weighted = weighted + jnp.sum(raised * prob_grad, axis=0, keepdims=True)
            e_s[pl.ds(i * step, step), :] = raised
            d_s[pl.ds(i * step, step), :] = prob_grad
        inverse = 1.0 / weight
        centre = weighted * inverse
        scaled = inverse * scale
        att_t = jnp.zeros((HD, bq), F32)
        qg_t = jnp.zeros((HD, bq), F32)
        for i in range(steps):
            at = pl.ds(i * step, step)
            raised = e_s[at, :]
            soft_low = (raised * inverse).astype(BF)
            score_grad = (raised * scaled * (d_s[at, :] - centre)).astype(BF)
            att_t = att_t + jnp.dot(vt[:, at], soft_low, preferred_element_type=F32)
            qg_t = qg_t + jnp.dot(kt[:, at], score_grad, preferred_element_type=F32)
            vacc[at, :] += jnp.dot(soft_low, g, preferred_element_type=F32)
            kacc[at, :] += jnp.dot(score_grad, q, preferred_element_type=F32)
        att[page, places, :] = att_t.T.astype(BF)
        qg[page, places, :] = qg_t.T.astype(BF)
        for z in range(ZN):
            to = block * ZN + z

            @pl.when(to != s)
            def _():
                out(0, page, to, s).start()
                out(1, page, to, s).start()

        @pl.when(at_block == blocks - 1)
        def _():
            kg[page] = kacc[pl.ds(0, lat), :].astype(BF)
            vg[page] = vacc[pl.ds(0, lat), :].astype(BF)
            columns = pl.ds(pl.multiple_of(page * lat, lat), lat)
            pg_t[pl.ds(0, HD), columns] = kacc[pl.ds(lat, lat), :].T.astype(BF)
            pg_t[pl.ds(HD, HD), columns] = vacc[pl.ds(lat, lat), :].T.astype(BF)

            @pl.when(page < pages - 1)
            def _():
                send_key_grads(page)

        return carry

    def send_key_grads(page):
        def one(k, carry):
            to = lax.rem(s + k, n)
            out(2, page, to, s).start()
            out(3, page, to, s).start()
            return carry

        lax.fori_loop(1, n, one, 0)

    lax.fori_loop(0, pages * blocks, one_block, 0)

    def mate(k):
        return high * group + lax.rem(j + k, group)

    def summed(t):
        columns = pl.ds(pl.multiple_of(t * chunk, chunk), chunk)
        return jnp.dot(pg_t[...], rows[:, columns], preferred_element_type=F32)

    def scatter(k):
        return push(
            outbound.at[k], parts.at[group - k], rsend.at[k], rrecv.at[k], "lang", mate(k)
        )

    def piece(t):
        return total.at[pl.ds(pl.multiple_of(t * chunk, chunk), chunk), :]

    def spread(k, t):
        return push(done, piece(t), asend.at[k], arecv.at[k], "lang", mate(k))

    fetch.wait()

    def one_part(k, carry):
        outbound[k] = summed(lax.rem(j + k, group)).astype(BF)
        scatter(k).start()
        return carry

    lax.fori_loop(1, group, one_part, 0)
    send_key_grads(pages - 1)
    own = []
    for i in range(4):
        own.append(
            pltpu.make_async_copy(
                sources[i].at[:, pl.ds(pl.multiple_of(s * part, part), part), :],
                landings[i].at[:, :, pl.ds(pl.multiple_of(s * HD, HD), HD)],
                own_sem.at[i],
            )
        )
        own[-1].start()
    acc = summed(j)
    for k in range(1, group):
        scatter(k).wait()
        acc = acc + parts[group - k].astype(F32)
    mine[...] = acc.astype(BF)
    cross = push(
        mine, pair, psend.at[0], precv.at[0], "lang", lax.rem(l + group, 2 * group)
    )
    cross.start()
    cross.wait()
    done[...] = (mine[...].astype(F32) + pair[...].astype(F32)).T.astype(BF)
    for k in range(1, group):
        spread(k, j).start()
    last = pltpu.make_async_copy(done, piece(j), own_sem.at[4])
    last.start()

    def ended(k, carry):
        other = lax.rem(s + k, n)
        for i in range(4):
            for page in range(pages):
                out(i, page, other, other).wait()
        return carry

    lax.fori_loop(1, n, ended, 0)
    for copy in own:
        copy.wait()
    last.wait()
    for k in range(1, group):
        spread(k, lax.rem(j + group - k, group)).wait()


def remote(body, number, out_shape, scratch, *operands, in_vmem=(), in_smem=()):
    return pl.pallas_call(
        body,
        out_shape=out_shape,
        in_specs=[
            pl.BlockSpec(memory_space=pltpu.SMEM)
            if i in in_smem
            else pl.BlockSpec(memory_space=pltpu.VMEM)
            if i in in_vmem
            else ANY
            for i in range(len(operands))
        ],
        out_specs=[ANY] * len(out_shape),
        scratch_shapes=scratch,
        compiler_params=pltpu.CompilerParams(
            collective_id=number, has_side_effects=True, vmem_limit_bytes=48 << 20
        ),
    )(*operands)


def local(
    prompt_rows,
    expert_ids,
    expert_gates,
    w_gate,
    w_up,
    w_down,
    w_kv,
    prompt_lengths,
    latent_q,
    latent_k,
    latent_v,
    grad_out,
):
    lang_count = lax.axis_size("lang")
    seq_count = lax.axis_size("seq")
    experts_all = lang_count
    rows_local, model_width = prompt_rows.shape
    ff = w_gate.shape[2]
    capacity = 3 * rows_local // experts_all
    sds = jax.ShapeDtypeStruct
    targets = slot_targets(expert_ids, experts_all, capacity)
    slot_ids = jnp.arange(experts_all * capacity, dtype=jnp.int32)
    dispatch_mask = jnp.any(slot_ids[:, None, None] == targets[None, :, :], axis=2).astype(BF)
    outgoing = jnp.dot(dispatch_mask, prompt_rows, preferred_element_type=F32).astype(BF)
    outgoing = outgoing.reshape(experts_all, capacity, model_width)
    pack = jnp.concatenate([w_gate[0].T, w_up[0].T, w_down[0]], axis=0)
    pages, part, _ = latent_q.shape
    lat = part * seq_count
    heads = sds((pages, lat, HD), BF)
    whole, arrived, qh, gh = remote(
        dispatch_kernel,
        1,
        [sds((3 * ff, model_width), BF), sds(outgoing.shape, BF), heads, heads],
        [
            DMA((1, lang_count)),
            DMA((1, lang_count)),
            DMA((2, seq_count)),
            DMA((2, seq_count)),
            DMA((4,)),
        ]
        + gather_sems(3),
        pack,
        outgoing,
        latent_q,
        grad_out,
    )
    tokens = arrived.reshape(experts_all * capacity, model_width)
    nt = (((1,), (1,)), ((), ()))
    gate_up = lax.dot_general(tokens, whole[: 2 * ff], nt, preferred_element_type=F32)
    hidden = (jax.nn.silu(gate_up[:, :ff]) * gate_up[:, ff:]).astype(BF)
    results = jnp.dot(hidden, whole[2 * ff :], preferred_element_type=F32).astype(BF)
    pick = (targets.T[:, :, None] == slot_ids[None, None, :]).astype(BF)
    group_rows, kh, vh = remote(
        prompt_kernel,
        3,
        [sds((rows_local * seq_count, model_width), BF)] + [heads] * 2,
        [
            pltpu.VMEM(outgoing.shape, BF),
            pltpu.VMEM((rows_local, model_width), BF),
            DMA((CHUNKS, lang_count)),
            DMA((CHUNKS, lang_count)),
            DMA((2, seq_count)),
            DMA((2, seq_count)),
            DMA((3 + CHUNKS,)),
        ]
        + gather_sems(CHUNKS),
        results.reshape(outgoing.shape),
        pick,
        expert_gates,
        latent_k,
        latent_v,
        in_vmem=(1, 2),
    )
    kv = jnp.dot(
        group_rows, w_kv.reshape(model_width, 2 * HD), preferred_element_type=F32
    ).astype(BF)
    half = lang_count // 2
    chunk = model_width // half
    bq = lat // YN
    att_rows, latent, total = remote(
        attend_kernel,
        4,
        [
            sds(latent_q.shape, BF),
            sds((3,) + latent_q.shape, BF),
            sds((model_width, 2 * HD), BF),
        ],
        [
            pltpu.VMEM(group_rows.shape, BF),
            pltpu.VMEM((pages, lat, HD), BF),
            pltpu.VMEM((pages, lat, HD), BF),
            pltpu.VMEM((pages, lat, HD), BF),
            pltpu.VMEM((pages, lat, HD), BF),
            pltpu.VMEM((2 * HD, pages * lat), BF),
            pltpu.VMEM((HD, 2 * lat), BF),
            pltpu.VMEM((HD, 2 * lat), BF),
            pltpu.VMEM((2 * lat, HD), F32),
            pltpu.VMEM((2 * lat, HD), F32),
            pltpu.VMEM((2 * lat, bq), F32),
            pltpu.VMEM((2 * lat, bq), F32),
            pltpu.VMEM((half, 2 * HD, chunk), BF),
            pltpu.VMEM((half, 2 * HD, chunk), BF),
            pltpu.VMEM((2 * HD, chunk), BF),
            pltpu.VMEM((2 * HD, chunk), BF),
            pltpu.VMEM((chunk, 2 * HD), BF),
            DMA((4, pages, seq_count)),
            DMA((4, pages, seq_count)),
            DMA((5,)),
            DMA((half,)),
            DMA((half,)),
            DMA((1,)),
            DMA((1,)),
            DMA((half,)),
            DMA((half,)),
        ],
        prompt_lengths,
        qh,
        gh,
        kh,
        vh,
        kv,
        group_rows,
        in_vmem=(1, 2, 3, 4, 5),
        in_smem=(0,),
    )
    grad_wkv = total.astype(F32).reshape(model_width, 2, HD)
    return (att_rows, latent, grad_wkv)


def solution(mesh):
    return jax.shard_map(
        local,
        mesh=mesh,
        in_specs=(
            P(("lang", "seq"), None),
            P(("lang", "seq"), None),
            P(("lang", "seq"), None),
            P("lang", "seq", None),
            P("lang", "seq", None),
            P("lang", None, "seq"),
            P(None, None, "seq"),
            P("lang"),
            P("lang", "seq", None),
            P("lang", "seq", None),
            P("lang", "seq", None),
            P("lang", "seq", None),
        ),
        out_specs=(P("lang", "seq", None), P(None, "lang", "seq", None), P(None, None, "seq")),
        check_vma=False,
    )
```

```python
import math

import jax
import jax.numpy as jnp
from jax import lax
from jax.experimental import pallas as pl
from jax.experimental.pallas import tpu as pltpu
from jax.sharding import PartitionSpec as P

HD = 128
MESH = pl.DeviceIdType.MESH
ANY = pl.BlockSpec(memory_space=pl.ANY)
BF = jnp.bfloat16
F32 = jnp.float32
DMA = pltpu.SemaphoreType.DMA
ZN = 4
CHUNKS = 2
YN = 4


def slot_targets(expert_ids, experts_all, capacity):
    rows_local, picks = expert_ids.shape
    flat_ids = expert_ids.reshape(rows_local * picks)
    expert_range = jnp.arange(experts_all, dtype=jnp.int32)
    onehot = (flat_ids[:, None] == expert_range[None, :]).astype(jnp.int32)
    earlier = jnp.cumsum(onehot, axis=0) - onehot
    slot_index = jnp.sum(earlier * onehot, axis=1)
    return (flat_ids * capacity + slot_index).reshape(rows_local, picks)


def push(src, dst, ssem, rsem, axis, target):
    return pltpu.make_async_remote_copy(
        src_ref=src,
        dst_ref=dst,
        send_sem=ssem,
        recv_sem=rsem,
        device_id={axis: target},
        device_id_type=MESH,
    )


def greet(axes):
    pl.semaphore_wait(pltpu.get_barrier_semaphore(), greet_all(axes))


def greet_all(axes):
    barrier = pltpu.get_barrier_semaphore()
    total = 0
    for axis in axes:
        count, of = everyone(axis)()

        def one(j, carry):
            pl.semaphore_signal(barrier, inc=1, device_id={axis: of(j)}, device_id_type=MESH)
            return carry

        lax.fori_loop(1, count, one, 0)
        total += count - 1
    return total


def everyone(axis):
    def make():
        n = lax.axis_size(axis)
        me = lax.axis_index(axis)
        return n, lambda j: lax.rem(me + j, n)

    return make


def ring_places():
    s = lax.axis_index("seq")
    y, z = lax.div(s, ZN), lax.rem(s, ZN)
    up = lax.rem(y + 1, YN) * ZN + z
    down = lax.rem(y + YN - 1, YN) * ZN + z
    return s, y, z, up, down


def gather_sems(chunks):
    return [DMA((chunks, ZN))] * 11


def gather_steps(source, view, sems):
    zl, zr, zin, us, ur, ds, dr, fus, fur, fds, fdr = sems
    s, y, z, up, down = ring_places()
    low_y = lax.rem(y + YN - 1, YN)
    high_y = lax.rem(y + 1, YN)

    def along(c, col, to_right, own):
        shard = y * ZN + col
        return push(
            source(c) if own else view(c, shard, None),
            view(c, shard, None),
            (zr if to_right else zl).at[c, col],
            zin.at[c, col],
            "seq",
            s + 1 if to_right else s - 1,
        )

    def across(c, col, own):
        shard = y * ZN + col
        src = source(c) if own else view(c, shard, None)
        dst = view(c, shard, None)
        return (
            push(src, dst, us.at[c, col], ur.at[c, col], "seq", up),
            push(src, dst, ds.at[c, col], dr.at[c, col], "seq", down),
        )

    def forwards(c, col):
        low = view(c, low_y * ZN + col, 0)
        high = view(c, high_y * ZN + col, 1)
        return (
            push(low, low, fus.at[c, col], fur.at[c, col], "seq", up),
            push(high, high, fds.at[c, col], fdr.at[c, col], "seq", down),
        )

    def pass_on(c, col):
        go_up, go_down = across(c, col, False)
        first, second = forwards(c, col)
        go_up.wait_recv()
        first.start()
        go_down.wait_recv()
        second.start()

    def each_side(t, do):
        @pl.when(z >= t)
        def _():
            do(z - t, True)

        @pl.when(z + t <= ZN - 1)
        def _():
            do(z + t, False)

    def on_way(to_right, do):
        @pl.when(z < ZN - 1 if to_right else z > 0)
        def _():
            do()

    def begin(c):
        for to_right in (True, False):
            on_way(to_right, lambda: along(c, z, to_right, True).start())
        for copy in across(c, z, True):
            copy.start()

    def step(c, t):
        def arrive(col, to_right):
            along(c, col, to_right, False).wait_recv()
            on_way(to_right, lambda: along(c, col, to_right, False).start())
            for copy in across(c, col, False):
                copy.start()

        each_side(t, arrive)

    def relay(c, t):
        if t == 0:
            pass_on(c, z)
        else:
            each_side(t, lambda col, to_right: pass_on(c, col))

    def landed(c):
        for col in range(ZN):
            for copy in forwards(c, col):
                copy.wait_recv()

    def finish(c):
        for col in range(ZN):
            for copy in across(c, col, False) + forwards(c, col):
                copy.wait_send()
        for to_right in (True, False):
            on_way(to_right, lambda: along(c, z, to_right, True).wait_send())
        for t in range(1, ZN):
            each_side(
                t,
                lambda col, to_right: on_way(
                    to_right, lambda: along(c, col, to_right, False).wait_send()
                ),
            )

    return begin, step, relay, landed, finish


def swap_steps(axis, pieces, send, recv):
    n = lax.axis_size(axis)
    me = lax.axis_index(axis)

    def copy(i, j):
        target = lax.rem(me + j, n)
        source, landing = pieces[i]
        return push(source(target), landing(me), send.at[i, j], recv.at[i, j], axis, target)

    def begin():
        def one(j, carry):
            for i in range(len(pieces)):
                copy(i, j).start()
            return carry

        lax.fori_loop(1, n, one, 0)

    def finish():
        def one(j, carry):
            for i in range(len(pieces)):
                copy(i, j).wait()
            return carry

        lax.fori_loop(1, n, one, 0)

    return begin, finish


def latent_pieces(pairs):
    part = pairs[0][0].shape[1]

    def source(array):
        return lambda t: array.at[:, :, pl.ds(pl.multiple_of(t * HD, HD), HD)]

    def landing(array):
        return lambda m: array.at[:, pl.ds(pl.multiple_of(m * part, part), part), :]

    return [(source(a), landing(b)) for a, b in pairs]


def encode(
    w_parts, outgoing, pick, gates, w_kv, latents, heads, kv, rows,
    whole, arrived, tokens, gate_up, hidden, results, returned, mixed,
    dsend, drecv, rsend, rrecv, lsend, lrecv, own_sem, wsems, msems,
):
    s = lax.axis_index("seq")
    me = lax.axis_index("lang")
    count, width = mixed.shape
    size = w_parts[0].shape[0]
    wide = width // CHUNKS
    experts, capacity, _ = arrived.shape

    def wview(c, shard, half):
        columns = pl.ds(pl.multiple_of(shard * HD, HD), HD)
        if half is None:
            return whole.at[pl.ds(c * size, size), columns]
        part = size // 2
        return whole.at[pl.ds(c * size + half * part, part), columns]

    def mview(c, shard, half):
        columns = pl.ds(c * wide, wide)
        if half is None:
            return rows.at[pl.ds(pl.multiple_of(shard * count, count), count), columns]
        part = count // 2
        at = pl.multiple_of(shard * count + half * part, part)
        return rows.at[pl.ds(at, part), columns]

    wbegin, wstep, wrelay, wlanded, wfinish = gather_steps(lambda c: w_parts[c], wview, wsems)
    begin, step, relay, landed, finish = gather_steps(
        lambda c: mixed.at[:, pl.ds(c * wide, wide)], mview, msems
    )
    dbegin, dfinish = swap_steps(
        "lang", [(lambda t: outgoing.at[t], lambda m: arrived.at[m])], dsend, drecv
    )
    pieces = latent_pieces(list(zip(latents, heads)))
    swaps = [
        swap_steps("seq", [pieces[i]], lsend.at[pl.ds(i, 1)], lrecv.at[pl.ds(i, 1)])
        for i in range(4)
    ]

    def back(c):
        columns = pl.ds(c * wide, wide)
        return swap_steps(
            "lang",
            [(lambda t: results.at[t, :, columns], lambda m: returned.at[m, :, columns])],
            rsend.at[pl.ds(c, 1)],
            rrecv.at[pl.ds(c, 1)],
        )

    backs = [back(c) for c in range(CHUNKS)]
    own = [pltpu.make_async_copy(outgoing.at[me], arrived.at[me], own_sem.at[0])]
    for c in range(3):
        own.append(pltpu.make_async_copy(w_parts[c], wview(c, s, None), own_sem.at[1 + c]))
    for i, (a, b) in enumerate(pieces):
        own.append(pltpu.make_async_copy(a(s), b(s), own_sem.at[4 + i]))
    for c in range(3):
        wbegin(c)
    dbegin()
    for copy in own:
        copy.start()
    for t in range(1, ZN):
        for c in range(3):
            wstep(c, t)
            wrelay(c, t - 1)
        if t == 1:
            swaps[0][0]()
            swaps[1][0]()
        if t == ZN - 1:
            swaps[2][0]()
            swaps[3][0]()
    for c in range(3):
        wrelay(c, ZN - 1)
    dfinish()
    for copy in own:
        copy.wait()
    for at in range(CHUNKS):
        columns = pl.ds(at * wide, wide)
        slots = arrived[:, :, columns].astype(F32)
        tokens[:, columns] = slots.reshape(experts * capacity, wide).astype(BF)
    wlanded(0)
    wlanded(1)
    gate_up[...] = jnp.zeros_like(gate_up)
    tile = 512

    def one_depth(i, carry):
        columns = pl.ds(pl.multiple_of(i * tile, tile), tile)
        gate_up[...] += lax.dot_general(
            tokens[:, columns],
            whole[pl.ds(0, 2 * size), columns],
            (((1,), (1,)), ((), ())),
            preferred_element_type=F32,
        )
        return carry

    lax.fori_loop(0, width // tile, one_depth, 0)
    gate = gate_up[:, :size]
    hidden[...] = (gate / (1.0 + jnp.exp(-gate)) * gate_up[:, size:]).astype(BF)
    wlanded(2)
    mates = []
    for c in range(CHUNKS):

        def one_tile(i, carry):
            columns = pl.ds(pl.multiple_of(c * wide + i * tile, tile), tile)
            result = jnp.dot(
                hidden[...], whole[pl.ds(2 * size, size), columns], preferred_element_type=F32
            )
            results[:, :, columns] = result.reshape(experts, capacity, tile).astype(BF)
            return carry

        lax.fori_loop(0, wide // tile, one_tile, 0)
        backs[c][0]()
        columns = pl.ds(c * wide, wide)
        mates.append(
            pltpu.make_async_copy(
                results.at[me, :, columns], returned.at[me, :, columns], own_sem.at[c]
            )
        )
        mates[-1].start()
    places = []

    def mix(c):
        backs[c][1]()
        mates[c].wait()
        columns = pl.ds(c * wide, wide)
        slots = returned[:, :, columns].astype(F32)
        slots = slots.reshape(experts * capacity, wide).astype(BF)
        total = jnp.zeros((count, wide), F32)
        for which in range(pick.shape[0]):
            picked = jnp.dot(pick[which], slots, preferred_element_type=F32)
            total = total + gates[:, which : which + 1] * picked
        mixed[:, columns] = total.astype(BF)
        place = pltpu.make_async_copy(
            mixed.at[:, columns], mview(c, s, None), own_sem.at[CHUNKS + c]
        )
        place.start()
        places.append(place)
        begin(c)

    mix(0)
    step(0, 1)
    mix(1)
    relay(0, 0)
    step(0, 2)
    step(1, 1)
    relay(0, 1)
    relay(1, 0)
    step(0, 3)
    step(1, 2)
    relay(0, 2)
    relay(1, 1)
    step(1, 3)
    relay(0, 3)
    relay(1, 2)
    relay(1, 3)
    for copy in places:
        copy.wait()
    for c in range(CHUNKS):
        landed(c)

    def one_part(i, carry):
        at = pl.ds(pl.multiple_of(i * 256, 256), 256)
        kv[at, :] = jnp.dot(rows[at, :], w_kv[...], preferred_element_type=F32).astype(BF)
        return carry

    lax.fori_loop(0, rows.shape[0] // 256, one_part, 0)
    for swap in swaps:
        swap[1]()
    for c in range(3):
        wfinish(c)
    for c in range(CHUNKS):
        finish(c)


def whole_kernel(*refs):
    refs = list(refs)

    def take(n):
        got = refs[:n]
        del refs[:n]
        return got

    (lengths, pick, gates, w_kv) = take(4)
    w_parts = take(3)
    (outgoing,) = take(1)
    latents = take(4)
    outs = take(3)
    heads = take(4)
    kv, rows = take(2)
    encode_scratch = take(8)
    encode_sems = take(7)
    wsems = take(11)
    msems = take(11)
    greet(["seq", "lang"])
    encode(
        w_parts, outgoing, pick, gates, w_kv, latents, heads, kv, rows,
        *encode_scratch, *encode_sems, wsems, msems,
    )
    q, k, v, g = heads
    attend(lengths, q, g, k, v, kv, rows, *outs, *refs)


def attend(
    lengths, q_ref, g_ref, k_ref, v_ref, kv_ref, rows, att_rows, latent, total,
    att, qg, kg, vg, pg_t, kt, vt, kacc, vacc, e_s, d_s,
    outbound, parts, mine, pair, done,
    send, recv, own_sem, rsend, rrecv, psend, precv, asend, arecv,
):
    s = lax.axis_index("seq")
    l = lax.axis_index("lang")
    n = lax.axis_size("seq")
    y = lax.div(s, ZN)
    group = lax.axis_size("lang") // 2
    high, j = lax.div(l, group), lax.rem(l, group)
    pages, lat, _ = q_ref.shape
    part = att_rows.shape[1]
    chunk = rows.shape[1] // group
    sources = [att, qg, kg, vg]
    landings = [att_rows, latent.at[0], latent.at[1], latent.at[2]]

    def out(i, page, to, frm):
        return push(
            sources[i].at[page, pl.ds(pl.multiple_of(to * part, part), part), :],
            landings[i].at[page, :, pl.ds(pl.multiple_of(frm * HD, HD), HD)],
            send.at[i, page, to],
            recv.at[i, page, frm],
            "seq",
            to,
        )

    step = 256
    blocks = YN
    bq = lat // blocks
    keys_all = 2 * lat
    steps = keys_all // step
    scale = 1.0 / math.sqrt(HD)
    to_two = scale * math.log2(math.e)
    nt = (((1,), (1,)), ((), ()))

    def one_block(turn, carry):
        page, at_block = lax.div(turn, blocks), lax.rem(turn, blocks)
        block = lax.rem(y + 1 + at_block, blocks)
        length = jnp.where(page == 0, lengths[0], lengths[1])

        def key_part(i):
            at = i * step
            if at < lat:
                return k_ref[page, pl.ds(at, step), :]
            return kv_ref[pl.ds(pl.multiple_of(page * lat + at - lat, step), step), pl.ds(0, HD)]

        def value_part(i):
            at = i * step
            if at < lat:
                return v_ref[page, pl.ds(at, step), :]
            return kv_ref[pl.ds(pl.multiple_of(page * lat + at - lat, step), step), pl.ds(HD, HD)]

        @pl.when(at_block == 0)
        def _():
            for i in range(steps):
                kt[:, pl.ds(i * step, step)] = key_part(i).T
                vt[:, pl.ds(i * step, step)] = value_part(i).T
            kacc[...] = jnp.zeros_like(kacc)
            vacc[...] = jnp.zeros_like(vacc)

        places = pl.ds(pl.multiple_of(block * bq, bq), bq)
        q, g = q_ref[page, places, :], g_ref[page, places, :]
        highest = jnp.full((1, bq), -jnp.inf, F32)
        for i in range(steps):
            scores = lax.dot_general(key_part(i), q, nt, preferred_element_type=F32)
            if i * step >= lat:
                at = i * step - lat + lax.broadcasted_iota(jnp.int32, (step, bq), 0)
                scores = jnp.where(at < length, scores, -jnp.inf)
            highest = jnp.maximum(highest, jnp.max(scores, axis=0, keepdims=True))
            e_s[pl.ds(i * step, step), :] = scores
        top = highest * to_two
        weight = jnp.zeros((1, bq), F32)
        weighted = jnp.zeros((1, bq), F32)
        for i in range(steps):
            raised = jnp.exp2(e_s[pl.ds(i * step, step), :] * to_two - top)
            prob_grad = lax.dot_general(value_part(i), g, nt, preferred_element_type=F32)
            weight = weight + jnp.sum(raised, axis=0, keepdims=True)
            weighted = weighted + jnp.sum(raised * prob_grad, axis=0, keepdims=True)
            e_s[pl.ds(i * step, step), :] = raised
            d_s[pl.ds(i * step, step), :] = prob_grad
        inverse = 1.0 / weight
        centre = weighted * inverse
        scaled = inverse * scale
        att_t = jnp.zeros((HD, bq), F32)
        qg_t = jnp.zeros((HD, bq), F32)
        for i in range(steps):
            at = pl.ds(i * step, step)
            raised = e_s[at, :]
            soft_low = (raised * inverse).astype(BF)
            score_grad = (raised * scaled * (d_s[at, :] - centre)).astype(BF)
            att_t = att_t + jnp.dot(vt[:, at], soft_low, preferred_element_type=F32)
            qg_t = qg_t + jnp.dot(kt[:, at], score_grad, preferred_element_type=F32)
            vacc[at, :] += jnp.dot(soft_low, g, preferred_element_type=F32)
            kacc[at, :] += jnp.dot(score_grad, q, preferred_element_type=F32)
        att[page, places, :] = att_t.T.astype(BF)
        qg[page, places, :] = qg_t.T.astype(BF)
        for z in range(ZN):
            to = block * ZN + z

            @pl.when(to != s)
            def _():
                out(0, page, to, s).start()
                out(1, page, to, s).start()

        @pl.when(at_block == blocks - 1)
        def _():
            kg[page] = kacc[pl.ds(0, lat), :].astype(BF)
            vg[page] = vacc[pl.ds(0, lat), :].astype(BF)
            columns = pl.ds(pl.multiple_of(page * lat, lat), lat)
            pg_t[pl.ds(0, HD), columns] = kacc[pl.ds(lat, lat), :].T.astype(BF)
            pg_t[pl.ds(HD, HD), columns] = vacc[pl.ds(lat, lat), :].T.astype(BF)

            @pl.when(page < pages - 1)
            def _():
                send_key_grads(page)

        return carry

    def send_key_grads(page):
        def one(k, carry):
            to = lax.rem(s + k, n)
            out(2, page, to, s).start()
            out(3, page, to, s).start()
            return carry

        lax.fori_loop(1, n, one, 0)

    lax.fori_loop(0, pages * blocks, one_block, 0)

    def mate(k):
        return high * group + lax.rem(j + k, group)

    def summed(t):
        columns = pl.ds(pl.multiple_of(t * chunk, chunk), chunk)
        return jnp.dot(pg_t[...], rows[:, columns], preferred_element_type=F32)

    def scatter(k):
        return push(
            outbound.at[k], parts.at[group - k], rsend.at[k], rrecv.at[k], "lang", mate(k)
        )

    def piece(t):
        return total.at[pl.ds(pl.multiple_of(t * chunk, chunk), chunk), :]

    def spread(k, t):
        return push(done, piece(t), asend.at[k], arecv.at[k], "lang", mate(k))

    def one_part(k, carry):
        outbound[k] = summed(lax.rem(j + k, group)).astype(BF)
        scatter(k).start()
        return carry

    lax.fori_loop(1, group, one_part, 0)
    send_key_grads(pages - 1)
    own = []
    for i in range(4):
        own.append(
            pltpu.make_async_copy(
                sources[i].at[:, pl.ds(pl.multiple_of(s * part, part), part), :],
                landings[i].at[:, :, pl.ds(pl.multiple_of(s * HD, HD), HD)],
                own_sem.at[i],
            )
        )
        own[-1].start()
    acc = summed(j)
    for k in range(1, group):
        scatter(k).wait()
        acc = acc + parts[group - k].astype(F32)
    mine[...] = acc.astype(BF)
    cross = push(
        mine, pair, psend.at[0], precv.at[0], "lang", lax.rem(l + group, 2 * group)
    )
    cross.start()
    cross.wait()
    done[...] = (mine[...].astype(F32) + pair[...].astype(F32)).T.astype(BF)
    for k in range(1, group):
        spread(k, j).start()
    last = pltpu.make_async_copy(done, piece(j), own_sem.at[4])
    last.start()

    def ended(k, carry):
        other = lax.rem(s + k, n)
        for i in range(4):
            for page in range(pages):
                out(i, page, other, other).wait()
        return carry

    lax.fori_loop(1, n, ended, 0)
    for copy in own:
        copy.wait()
    last.wait()
    for k in range(1, group):
        spread(k, lax.rem(j + group - k, group)).wait()


def remote(body, number, out_shape, scratch, *operands, in_vmem=(), in_smem=()):
    return pl.pallas_call(
        body,
        out_shape=out_shape,
        in_specs=[
            pl.BlockSpec(memory_space=pltpu.SMEM)
            if i in in_smem
            else pl.BlockSpec(memory_space=pltpu.VMEM)
            if i in in_vmem
            else ANY
            for i in range(len(operands))
        ],
        out_specs=[ANY] * len(out_shape),
        scratch_shapes=scratch,
        compiler_params=pltpu.CompilerParams(
            collective_id=number, has_side_effects=True, vmem_limit_bytes=60 << 20
        ),
    )(*operands)


def local(
    prompt_rows,
    expert_ids,
    expert_gates,
    w_gate,
    w_up,
    w_down,
    w_kv,
    prompt_lengths,
    latent_q,
    latent_k,
    latent_v,
    grad_out,
):
    lang_count = lax.axis_size("lang")
    seq_count = lax.axis_size("seq")
    experts_all = lang_count
    rows_local, model_width = prompt_rows.shape
    ff = w_gate.shape[2]
    capacity = 3 * rows_local // experts_all
    sds = jax.ShapeDtypeStruct
    targets = slot_targets(expert_ids, experts_all, capacity)
    slot_ids = jnp.arange(experts_all * capacity, dtype=jnp.int32)
    dispatch_mask = jnp.any(slot_ids[:, None, None] == targets[None, :, :], axis=2).astype(BF)
    outgoing = jnp.dot(dispatch_mask, prompt_rows, preferred_element_type=F32).astype(BF)
    outgoing = outgoing.reshape(experts_all, capacity, model_width)
    pick = (targets.T[:, :, None] == slot_ids[None, None, :]).astype(BF)
    pages, part, _ = latent_q.shape
    lat = part * seq_count
    half = lang_count // 2
    chunk = model_width // half
    bq = lat // YN
    slots = experts_all * capacity
    att_rows, latent, total = remote(
        whole_kernel,
        1,
        [
            sds(latent_q.shape, BF),
            sds((3,) + latent_q.shape, BF),
            sds((model_width, 2 * HD), BF),
        ],
        [pltpu.VMEM((pages, lat, HD), BF)] * 4
        + [
            pltpu.VMEM((pages * lat, 2 * HD), BF),
            pltpu.VMEM((rows_local * seq_count, model_width), BF),
            pltpu.VMEM((3 * ff, model_width), BF),
            pltpu.VMEM(outgoing.shape, BF),
            pltpu.VMEM((slots, model_width), BF),
            pltpu.VMEM((slots, 2 * ff), F32),
            pltpu.VMEM((slots, ff), BF),
            pltpu.VMEM(outgoing.shape, BF),
            pltpu.VMEM(outgoing.shape, BF),
            pltpu.VMEM((rows_local, model_width), BF),
            DMA((1, lang_count)),
            DMA((1, lang_count)),
            DMA((CHUNKS, lang_count)),
            DMA((CHUNKS, lang_count)),
            DMA((4, seq_count)),
            DMA((4, seq_count)),
            DMA((8,)),
        ]
        + gather_sems(3)
        + gather_sems(CHUNKS)
        + [pltpu.VMEM((pages, lat, HD), BF)] * 4
        + [
            pltpu.VMEM((2 * HD, pages * lat), BF),
            pltpu.VMEM((HD, 2 * lat), BF),
            pltpu.VMEM((HD, 2 * lat), BF),
            pltpu.VMEM((2 * lat, HD), F32),
            pltpu.VMEM((2 * lat, HD), F32),
            pltpu.VMEM((2 * lat, bq), F32),
            pltpu.VMEM((2 * lat, bq), F32),
            pltpu.VMEM((half, 2 * HD, chunk), BF),
            pltpu.VMEM((half, 2 * HD, chunk), BF),
            pltpu.VMEM((2 * HD, chunk), BF),
            pltpu.VMEM((2 * HD, chunk), BF),
            pltpu.VMEM((chunk, 2 * HD), BF),
            DMA((4, pages, seq_count)),
            DMA((4, pages, seq_count)),
            DMA((5,)),
            DMA((half,)),
            DMA((half,)),
            DMA((1,)),
            DMA((1,)),
            DMA((half,)),
            DMA((half,)),
        ],
        prompt_lengths,
        pick,
        expert_gates,
        w_kv.reshape(model_width, 2 * HD),
        w_gate[0].T,
        w_up[0].T,
        w_down[0],
        outgoing,
        latent_q,
        latent_k,
        latent_v,
        grad_out,
        in_vmem=(1, 2, 3),
        in_smem=(0,),
    )
    grad_wkv = total.astype(F32).reshape(model_width, 2, HD)
    return (att_rows, latent, grad_wkv)


def solution(mesh):
    return jax.shard_map(
        local,
        mesh=mesh,
        in_specs=(
            P(("lang", "seq"), None),
            P(("lang", "seq"), None),
            P(("lang", "seq"), None),
            P("lang", "seq", None),
            P("lang", "seq", None),
            P("lang", None, "seq"),
            P(None, None, "seq"),
            P("lang"),
            P("lang", "seq", None),
            P("lang", "seq", None),
            P("lang", "seq", None),
            P("lang", "seq", None),
        ),
        out_specs=(P("lang", "seq", None), P(None, "lang", "seq", None), P(None, None, "seq")),
        check_vma=False,
    )
```

```python
import math

import jax
import jax.numpy as jnp
from jax import lax
from jax.experimental import pallas as pl
from jax.experimental.pallas import tpu as pltpu
from jax.sharding import PartitionSpec as P

HD = 128
MESH = pl.DeviceIdType.MESH
ANY = pl.BlockSpec(memory_space=pl.ANY)
BF = jnp.bfloat16
F32 = jnp.float32
DMA = pltpu.SemaphoreType.DMA
ZN = 4
CHUNKS = 2
YN = 4


def push(src, dst, ssem, rsem, axis, target):
    return pltpu.make_async_remote_copy(
        src_ref=src,
        dst_ref=dst,
        send_sem=ssem,
        recv_sem=rsem,
        device_id={axis: target},
        device_id_type=MESH,
    )


def greet(axes):
    pl.semaphore_wait(pltpu.get_barrier_semaphore(), greet_all(axes))


def greet_all(axes):
    barrier = pltpu.get_barrier_semaphore()
    total = 0
    for axis in axes:
        count, of = everyone(axis)()

        def one(j, carry):
            pl.semaphore_signal(barrier, inc=1, device_id={axis: of(j)}, device_id_type=MESH)
            return carry

        lax.fori_loop(1, count, one, 0)
        total += count - 1
    return total


def everyone(axis):
    def make():
        n = lax.axis_size(axis)
        me = lax.axis_index(axis)
        return n, lambda j: lax.rem(me + j, n)

    return make


def ring_places():
    s = lax.axis_index("seq")
    y, z = lax.div(s, ZN), lax.rem(s, ZN)
    up = lax.rem(y + 1, YN) * ZN + z
    down = lax.rem(y + YN - 1, YN) * ZN + z
    return s, y, z, up, down


def gather_sems(chunks):
    return [DMA((chunks, ZN))] * 11


def gather_steps(source, view, sems):
    zl, zr, zin, us, ur, ds, dr, fus, fur, fds, fdr = sems
    s, y, z, up, down = ring_places()
    low_y = lax.rem(y + YN - 1, YN)
    high_y = lax.rem(y + 1, YN)

    def along(c, col, to_right, own):
        shard = y * ZN + col
        return push(
            source(c) if own else view(c, shard, None),
            view(c, shard, None),
            (zr if to_right else zl).at[c, col],
            zin.at[c, col],
            "seq",
            s + 1 if to_right else s - 1,
        )

    def across(c, col, own):
        shard = y * ZN + col
        src = source(c) if own else view(c, shard, None)
        dst = view(c, shard, None)
        return (
            push(src, dst, us.at[c, col], ur.at[c, col], "seq", up),
            push(src, dst, ds.at[c, col], dr.at[c, col], "seq", down),
        )

    def forwards(c, col):
        low = view(c, low_y * ZN + col, 0)
        high = view(c, high_y * ZN + col, 1)
        return (
            push(low, low, fus.at[c, col], fur.at[c, col], "seq", up),
            push(high, high, fds.at[c, col], fdr.at[c, col], "seq", down),
        )

    def pass_on(c, col):
        go_up, go_down = across(c, col, False)
        first, second = forwards(c, col)
        go_up.wait_recv()
        first.start()
        go_down.wait_recv()
        second.start()

    def each_side(t, do):
        @pl.when(z >= t)
        def _():
            do(z - t, True)

        @pl.when(z + t <= ZN - 1)
        def _():
            do(z + t, False)

    def on_way(to_right, do):
        @pl.when(z < ZN - 1 if to_right else z > 0)
        def _():
            do()

    def begin(c):
        for to_right in (True, False):
            on_way(to_right, lambda: along(c, z, to_right, True).start())
        for copy in across(c, z, True):
            copy.start()

    def step(c, t):
        def arrive(col, to_right):
            along(c, col, to_right, False).wait_recv()
            on_way(to_right, lambda: along(c, col, to_right, False).start())
            for copy in across(c, col, False):
                copy.start()

        each_side(t, arrive)

    def relay(c, t):
        if t == 0:
            pass_on(c, z)
        else:
            each_side(t, lambda col, to_right: pass_on(c, col))

    def landed(c):
        for col in range(ZN):
            for copy in forwards(c, col):
                copy.wait_recv()

    def finish(c):
        for col in range(ZN):
            for copy in across(c, col, False) + forwards(c, col):
                copy.wait_send()
        for to_right in (True, False):
            on_way(to_right, lambda: along(c, z, to_right, True).wait_send())
        for t in range(1, ZN):
            each_side(
                t,
                lambda col, to_right: on_way(
                    to_right, lambda: along(c, col, to_right, False).wait_send()
                ),
            )

    return begin, step, relay, landed, finish


def swap_steps(axis, pieces, send, recv):
    n = lax.axis_size(axis)
    me = lax.axis_index(axis)

    def copy(i, j):
        target = lax.rem(me + j, n)
        source, landing = pieces[i]
        return push(source(target), landing(me), send.at[i, j], recv.at[i, j], axis, target)

    def begin():
        def one(j, carry):
            for i in range(len(pieces)):
                copy(i, j).start()
            return carry

        lax.fori_loop(1, n, one, 0)

    def finish():
        def one(j, carry):
            for i in range(len(pieces)):
                copy(i, j).wait()
            return carry

        lax.fori_loop(1, n, one, 0)

    return begin, finish


def latent_pieces(pairs):
    part = pairs[0][0].shape[1]

    def source(array):
        return lambda t: array.at[:, :, pl.ds(pl.multiple_of(t * HD, HD), HD)]

    def landing(array):
        return lambda m: array.at[:, pl.ds(pl.multiple_of(m * part, part), part), :]

    return [(source(a), landing(b)) for a, b in pairs]


def route(ids, gates, prompt_rows, masks, gate_columns, outgoing):
    experts, capacity, width = outgoing.shape
    count = prompt_rows.shape[0]
    expert = lax.broadcasted_iota(jnp.int32, (experts, count), 0)
    chosen = [expert == ids[k : k + 1, :] for k in range(2)]
    named = jnp.where(jnp.logical_or(chosen[0], chosen[1]), 1.0, 0.0).astype(BF)
    ahead = lax.broadcasted_iota(jnp.int32, (count, count), 0)
    ahead = ahead < lax.broadcasted_iota(jnp.int32, (count, count), 1)
    ahead = jnp.where(ahead, 1.0, 0.0).astype(BF)
    earlier = jnp.dot(named, ahead, preferred_element_type=F32)
    slot = lax.broadcasted_iota(jnp.int32, (experts * capacity, count), 0)
    both = jnp.zeros((experts * capacity, count), F32)
    for k in range(2):
        order = jnp.sum(jnp.where(chosen[k], earlier, 0.0), axis=0, keepdims=True)
        target = ids[k : k + 1, :] * capacity + order.astype(jnp.int32)
        mask = jnp.where(slot == target, 1.0, 0.0)
        masks[k] = mask.astype(BF)
        both = both + mask
        gate_columns[k] = jnp.broadcast_to(gates[k : k + 1, :], (count, count)).T
    both = both.astype(BF)
    tile = 512
    for i in range(width // tile):
        columns = pl.ds(i * tile, tile)
        sent = jnp.dot(both, prompt_rows[:, columns], preferred_element_type=F32)
        outgoing[:, :, columns] = sent.reshape(experts, capacity, tile).astype(BF)


def encode(
    w_parts, prompt_rows, ids, gates, w_kv, latents, heads, kv, rows,
    masks, gate_columns, outgoing, whole, arrived, tokens, gate_up, hidden, results, returned, mixed,
    dsend, drecv, rsend, rrecv, lsend, lrecv, own_sem, wsems, msems,
):
    s = lax.axis_index("seq")
    me = lax.axis_index("lang")
    count, width = mixed.shape
    size = w_parts[0].shape[0]
    wide = width // CHUNKS
    experts, capacity, _ = arrived.shape

    def wview(c, shard, half):
        columns = pl.ds(pl.multiple_of(shard * HD, HD), HD)
        if half is None:
            return whole.at[pl.ds(c * size, size), columns]
        part = size // 2
        return whole.at[pl.ds(c * size + half * part, part), columns]

    def mview(c, shard, half):
        columns = pl.ds(c * wide, wide)
        if half is None:
            return rows.at[pl.ds(pl.multiple_of(shard * count, count), count), columns]
        part = count // 2
        at = pl.multiple_of(shard * count + half * part, part)
        return rows.at[pl.ds(at, part), columns]

    wbegin, wstep, wrelay, wlanded, wfinish = gather_steps(lambda c: w_parts[c], wview, wsems)
    begin, step, relay, landed, finish = gather_steps(
        lambda c: mixed.at[:, pl.ds(c * wide, wide)], mview, msems
    )
    dbegin, dfinish = swap_steps(
        "lang", [(lambda t: outgoing.at[t], lambda m: arrived.at[m])], dsend, drecv
    )
    pieces = latent_pieces(list(zip(latents, heads)))
    swaps = [
        swap_steps("seq", [pieces[i]], lsend.at[pl.ds(i, 1)], lrecv.at[pl.ds(i, 1)])
        for i in range(4)
    ]

    def back(c):
        columns = pl.ds(c * wide, wide)
        return swap_steps(
            "lang",
            [(lambda t: results.at[t, :, columns], lambda m: returned.at[m, :, columns])],
            rsend.at[pl.ds(c, 1)],
            rrecv.at[pl.ds(c, 1)],
        )

    backs = [back(c) for c in range(CHUNKS)]
    own = [pltpu.make_async_copy(outgoing.at[me], arrived.at[me], own_sem.at[0])]
    for c in range(3):
        own.append(pltpu.make_async_copy(w_parts[c], wview(c, s, None), own_sem.at[1 + c]))
    for i, (a, b) in enumerate(pieces):
        own.append(pltpu.make_async_copy(a(s), b(s), own_sem.at[4 + i]))
    for c in range(3):
        wbegin(c)
    for copy in own[1:]:
        copy.start()
    route(ids, gates, prompt_rows, masks, gate_columns, outgoing)
    own[0].start()
    for t in range(1, ZN):
        for c in range(3):
            wstep(c, t)
            wrelay(c, t - 1)
        if t == 1:
            dbegin()
        if t == 2:
            swaps[0][0]()
        if t == ZN - 1:
            swaps[1][0]()
            swaps[2][0]()
    for c in range(3):
        wrelay(c, ZN - 1)
    dfinish()
    for copy in own:
        copy.wait()
    for at in range(CHUNKS):
        columns = pl.ds(at * wide, wide)
        slots = arrived[:, :, columns].astype(F32)
        tokens[:, columns] = slots.reshape(experts * capacity, wide).astype(BF)
    wlanded(0)
    wlanded(1)
    gate_up[...] = jnp.zeros_like(gate_up)
    tile = 512

    def one_depth(i, carry):
        columns = pl.ds(pl.multiple_of(i * tile, tile), tile)
        gate_up[...] += lax.dot_general(
            tokens[:, columns],
            whole[pl.ds(0, 2 * size), columns],
            (((1,), (1,)), ((), ())),
            preferred_element_type=F32,
        )
        return carry

    lax.fori_loop(0, width // tile, one_depth, 0)
    gate = gate_up[:, :size]
    hidden[...] = (gate / (1.0 + jnp.exp(-gate)) * gate_up[:, size:]).astype(BF)
    wlanded(2)
    mates = []
    for c in range(CHUNKS):

        def one_tile(i, carry):
            columns = pl.ds(pl.multiple_of(c * wide + i * tile, tile), tile)
            result = jnp.dot(
                hidden[...], whole[pl.ds(2 * size, size), columns], preferred_element_type=F32
            )
            results[:, :, columns] = result.reshape(experts, capacity, tile).astype(BF)
            return carry

        lax.fori_loop(0, wide // tile, one_tile, 0)
        backs[c][0]()
        columns = pl.ds(c * wide, wide)
        mates.append(
            pltpu.make_async_copy(
                results.at[me, :, columns], returned.at[me, :, columns], own_sem.at[c]
            )
        )
        mates[-1].start()
    places = []

    def mix(c):
        backs[c][1]()
        mates[c].wait()
        columns = pl.ds(c * wide, wide)
        slots = returned[:, :, columns].astype(F32)
        slots = slots.reshape(experts * capacity, wide).astype(BF)
        total = jnp.zeros((count, wide), F32)
        for which in range(masks.shape[0]):
            picked = lax.dot_general(
                masks[which], slots, (((0,), (0,)), ((), ())), preferred_element_type=F32
            )
            total = total + gate_columns[which][:, 0:1] * picked
        mixed[:, columns] = total.astype(BF)
        place = pltpu.make_async_copy(
            mixed.at[:, columns], mview(c, s, None), own_sem.at[CHUNKS + c]
        )
        place.start()
        places.append(place)
        begin(c)

    for tick in range(CHUNKS + ZN):
        if tick < CHUNKS:
            mix(tick)
        for c in range(CHUNKS):
            if 0 <= tick - c - 1 < ZN:
                relay(c, tick - c - 1)
        for c in range(CHUNKS):
            if 1 <= tick - c + 1 < ZN:
                step(c, tick - c + 1)
        if tick == CHUNKS + 1:
            swaps[3][0]()
    for copy in places:
        copy.wait()
    for c in range(CHUNKS):
        landed(c)

    def one_part(i, carry):
        at = pl.ds(pl.multiple_of(i * 256, 256), 256)
        kv[at, :] = jnp.dot(rows[at, :], w_kv[...], preferred_element_type=F32).astype(BF)
        return carry

    lax.fori_loop(0, rows.shape[0] // 256, one_part, 0)
    for swap in swaps:
        swap[1]()
    for c in range(3):
        wfinish(c)
    for c in range(CHUNKS):
        finish(c)


def whole_kernel(*refs):
    refs = list(refs)

    def take(n):
        got = refs[:n]
        del refs[:n]
        return got

    (lengths, ids, gates, w_kv, prompt_rows) = take(5)
    w_parts = take(3)
    latents = take(4)
    outs = take(3)
    heads = take(4)
    kv, rows = take(2)
    encode_scratch = take(11)
    encode_sems = take(7)
    wsems = take(11)
    msems = take(11)
    greet(["seq", "lang"])
    encode(
        w_parts, prompt_rows, ids, gates, w_kv, latents, heads, kv, rows,
        *encode_scratch, *encode_sems, wsems, msems,
    )
    q, k, v, g = heads
    attend(lengths, q, g, k, v, kv, rows, *outs, *refs)


def attend(
    lengths, q_ref, g_ref, k_ref, v_ref, kv_ref, rows, att_rows, latent, total,
    att, qg, kg, vg, pg_t, kt, vt, kacc, vacc, e_s, d_s,
    outbound, parts, mine, pair, done,
    send, recv, own_sem, rsend, rrecv, psend, precv, asend, arecv,
):
    s = lax.axis_index("seq")
    l = lax.axis_index("lang")
    n = lax.axis_size("seq")
    y = lax.div(s, ZN)
    group = lax.axis_size("lang") // 2
    high, j = lax.div(l, group), lax.rem(l, group)
    pages, lat, _ = q_ref.shape
    part = att_rows.shape[1]
    chunk = rows.shape[1] // group
    sources = [att, qg, kg, vg]
    landings = [att_rows, latent.at[0], latent.at[1], latent.at[2]]

    def out(i, page, to, frm):
        return push(
            sources[i].at[page, pl.ds(pl.multiple_of(to * part, part), part), :],
            landings[i].at[page, :, pl.ds(pl.multiple_of(frm * HD, HD), HD)],
            send.at[i, page, to],
            recv.at[i, page, frm],
            "seq",
            to,
        )

    step = 256
    blocks = YN
    bq = lat // blocks
    keys_all = 2 * lat
    steps = keys_all // step
    scale = 1.0 / math.sqrt(HD)
    to_two = scale * math.log2(math.e)
    nt = (((1,), (1,)), ((), ()))

    def one_block(turn, carry):
        page, at_block = lax.div(turn, blocks), lax.rem(turn, blocks)
        block = lax.rem(y + 1 + at_block, blocks)
        length = jnp.where(page == 0, lengths[0], lengths[1])

        def key_part(i):
            at = i * step
            if at < lat:
                return k_ref[page, pl.ds(at, step), :]
            return kv_ref[pl.ds(pl.multiple_of(page * lat + at - lat, step), step), pl.ds(0, HD)]

        def value_part(i):
            at = i * step
            if at < lat:
                return v_ref[page, pl.ds(at, step), :]
            return kv_ref[pl.ds(pl.multiple_of(page * lat + at - lat, step), step), pl.ds(HD, HD)]

        @pl.when(at_block == 0)
        def _():
            for i in range(steps):
                kt[:, pl.ds(i * step, step)] = key_part(i).T
                vt[:, pl.ds(i * step, step)] = value_part(i).T
            kacc[...] = jnp.zeros_like(kacc)
            vacc[...] = jnp.zeros_like(vacc)

        places = pl.ds(pl.multiple_of(block * bq, bq), bq)
        q, g = q_ref[page, places, :], g_ref[page, places, :]
        highest = jnp.full((1, bq), -jnp.inf, F32)
        for i in range(steps):
            scores = lax.dot_general(key_part(i), q, nt, preferred_element_type=F32)
            if i * step >= lat:
                at = i * step - lat + lax.broadcasted_iota(jnp.int32, (step, bq), 0)
                scores = jnp.where(at < length, scores, -jnp.inf)
            highest = jnp.maximum(highest, jnp.max(scores, axis=0, keepdims=True))
            e_s[pl.ds(i * step, step), :] = scores
        top = highest * to_two
        weight = jnp.zeros((1, bq), F32)
        weighted = jnp.zeros((1, bq), F32)
        for i in range(steps):
            raised = jnp.exp2(e_s[pl.ds(i * step, step), :] * to_two - top)
            prob_grad = lax.dot_general(value_part(i), g, nt, preferred_element_type=F32)
            weight = weight + jnp.sum(raised, axis=0, keepdims=True)
            weighted = weighted + jnp.sum(raised * prob_grad, axis=0, keepdims=True)
            e_s[pl.ds(i * step, step), :] = raised
            d_s[pl.ds(i * step, step), :] = prob_grad
        inverse = 1.0 / weight
        centre = weighted * inverse
        scaled = inverse * scale
        att_t = jnp.zeros((HD, bq), F32)
        qg_t = jnp.zeros((HD, bq), F32)
        for i in range(steps):
            at = pl.ds(i * step, step)
            raised = e_s[at, :]
            soft_low = (raised * inverse).astype(BF)
            score_grad = (raised * scaled * (d_s[at, :] - centre)).astype(BF)
            att_t = att_t + jnp.dot(vt[:, at], soft_low, preferred_element_type=F32)
            qg_t = qg_t + jnp.dot(kt[:, at], score_grad, preferred_element_type=F32)
            vacc[at, :] += jnp.dot(soft_low, g, preferred_element_type=F32)
            kacc[at, :] += jnp.dot(score_grad, q, preferred_element_type=F32)
        att[page, places, :] = att_t.T.astype(BF)
        qg[page, places, :] = qg_t.T.astype(BF)
        for z in range(ZN):
            to = block * ZN + z

            @pl.when(to != s)
            def _():
                out(0, page, to, s).start()
                out(1, page, to, s).start()

        @pl.when(at_block == blocks - 1)
        def _():
            kg[page] = kacc[pl.ds(0, lat), :].astype(BF)
            vg[page] = vacc[pl.ds(0, lat), :].astype(BF)
            columns = pl.ds(pl.multiple_of(page * lat, lat), lat)
            pg_t[pl.ds(0, HD), columns] = kacc[pl.ds(lat, lat), :].T.astype(BF)
            pg_t[pl.ds(HD, HD), columns] = vacc[pl.ds(lat, lat), :].T.astype(BF)

            @pl.when(page < pages - 1)
            def _():
                send_key_grads(page)

        return carry

    def send_key_grads(page):
        def one(k, carry):
            to = lax.rem(s + k, n)
            out(2, page, to, s).start()
            out(3, page, to, s).start()
            return carry

        lax.fori_loop(1, n, one, 0)

    lax.fori_loop(0, pages * blocks, one_block, 0)

    def mate(k):
        return high * group + lax.rem(j + k, group)

    def summed(t):
        columns = pl.ds(pl.multiple_of(t * chunk, chunk), chunk)
        return jnp.dot(pg_t[...], rows[:, columns], preferred_element_type=F32)

    def scatter(k):
        return push(
            outbound.at[k], parts.at[group - k], rsend.at[k], rrecv.at[k], "lang", mate(k)
        )

    def piece(t):
        return total.at[pl.ds(pl.multiple_of(t * chunk, chunk), chunk), :]

    def spread(k, t):
        return push(done, piece(t), asend.at[k], arecv.at[k], "lang", mate(k))

    def one_part(k, carry):
        outbound[k] = summed(lax.rem(j + k, group)).astype(BF)
        scatter(k).start()
        return carry

    lax.fori_loop(1, group, one_part, 0)
    send_key_grads(pages - 1)
    own = []
    for i in range(4):
        own.append(
            pltpu.make_async_copy(
                sources[i].at[:, pl.ds(pl.multiple_of(s * part, part), part), :],
                landings[i].at[:, :, pl.ds(pl.multiple_of(s * HD, HD), HD)],
                own_sem.at[i],
            )
        )
        own[-1].start()
    acc = summed(j)
    for k in range(1, group):
        scatter(k).wait()
        acc = acc + parts[group - k].astype(F32)
    mine[...] = acc.astype(BF)
    cross = push(
        mine, pair, psend.at[0], precv.at[0], "lang", lax.rem(l + group, 2 * group)
    )
    cross.start()
    cross.wait()
    done[...] = (mine[...].astype(F32) + pair[...].astype(F32)).T.astype(BF)
    for k in range(1, group):
        spread(k, j).start()
    last = pltpu.make_async_copy(done, piece(j), own_sem.at[4])
    last.start()

    def ended(k, carry):
        other = lax.rem(s + k, n)
        for i in range(4):
            for page in range(pages):
                out(i, page, other, other).wait()
        return carry

    lax.fori_loop(1, n, ended, 0)
    for copy in own:
        copy.wait()
    last.wait()
    for k in range(1, group):
        spread(k, lax.rem(j + group - k, group)).wait()


def remote(body, number, out_shape, scratch, *operands, in_vmem=(), in_smem=()):
    return pl.pallas_call(
        body,
        out_shape=out_shape,
        in_specs=[
            pl.BlockSpec(memory_space=pltpu.SMEM)
            if i in in_smem
            else pl.BlockSpec(memory_space=pltpu.VMEM)
            if i in in_vmem
            else ANY
            for i in range(len(operands))
        ],
        out_specs=[ANY] * len(out_shape),
        scratch_shapes=scratch,
        compiler_params=pltpu.CompilerParams(
            collective_id=number, has_side_effects=True, vmem_limit_bytes=60 << 20
        ),
    )(*operands)


def local(
    prompt_rows,
    expert_ids,
    expert_gates,
    w_gate,
    w_up,
    w_down,
    w_kv,
    prompt_lengths,
    latent_q,
    latent_k,
    latent_v,
    grad_out,
):
    lang_count = lax.axis_size("lang")
    seq_count = lax.axis_size("seq")
    experts_all = lang_count
    rows_local, model_width = prompt_rows.shape
    ff = w_gate.shape[2]
    capacity = 3 * rows_local // experts_all
    sds = jax.ShapeDtypeStruct
    pages, part, _ = latent_q.shape
    lat = part * seq_count
    half = lang_count // 2
    chunk = model_width // half
    bq = lat // YN
    slots = experts_all * capacity
    blocks = (experts_all, capacity, model_width)
    att_rows, latent, total = remote(
        whole_kernel,
        1,
        [
            sds(latent_q.shape, BF),
            sds((3,) + latent_q.shape, BF),
            sds((model_width, 2 * HD), BF),
        ],
        [pltpu.VMEM((pages, lat, HD), BF)] * 4
        + [
            pltpu.VMEM((pages * lat, 2 * HD), BF),
            pltpu.VMEM((rows_local * seq_count, model_width), BF),
            pltpu.VMEM((2, slots, rows_local), BF),
            pltpu.VMEM((2, rows_local, rows_local), F32),
            pltpu.VMEM(blocks, BF),
            pltpu.VMEM((3 * ff, model_width), BF),
            pltpu.VMEM(blocks, BF),
            pltpu.VMEM((slots, model_width), BF),
            pltpu.VMEM((slots, 2 * ff), F32),
            pltpu.VMEM((slots, ff), BF),
            pltpu.VMEM(blocks, BF),
            pltpu.VMEM(blocks, BF),
            pltpu.VMEM((rows_local, model_width), BF),
            DMA((1, lang_count)),
            DMA((1, lang_count)),
            DMA((CHUNKS, lang_count)),
            DMA((CHUNKS, lang_count)),
            DMA((4, seq_count)),
            DMA((4, seq_count)),
            DMA((8,)),
        ]
        + gather_sems(3)
        + gather_sems(CHUNKS)
        + [pltpu.VMEM((pages, lat, HD), BF)] * 4
        + [
            pltpu.VMEM((2 * HD, pages * lat), BF),
            pltpu.VMEM((HD, 2 * lat), BF),
            pltpu.VMEM((HD, 2 * lat), BF),
            pltpu.VMEM((2 * lat, HD), F32),
            pltpu.VMEM((2 * lat, HD), F32),
            pltpu.VMEM((2 * lat, bq), F32),
            pltpu.VMEM((2 * lat, bq), F32),
            pltpu.VMEM((half, 2 * HD, chunk), BF),
            pltpu.VMEM((half, 2 * HD, chunk), BF),
            pltpu.VMEM((2 * HD, chunk), BF),
            pltpu.VMEM((2 * HD, chunk), BF),
            pltpu.VMEM((chunk, 2 * HD), BF),
            DMA((4, pages, seq_count)),
            DMA((4, pages, seq_count)),
            DMA((5,)),
            DMA((half,)),
            DMA((half,)),
            DMA((1,)),
            DMA((1,)),
            DMA((half,)),
            DMA((half,)),
        ],
        prompt_lengths,
        expert_ids.T,
        expert_gates.T,
        w_kv.reshape(model_width, 2 * HD),
        prompt_rows,
        w_gate[0].T,
        w_up[0].T,
        w_down[0],
        latent_q,
        latent_k,
        latent_v,
        grad_out,
        in_vmem=(1, 2, 3, 4),
        in_smem=(0,),
    )
    grad_wkv = total.astype(F32).reshape(model_width, 2, HD)
    return (att_rows, latent, grad_wkv)


def solution(mesh):
    return jax.shard_map(
        local,
        mesh=mesh,
        in_specs=(
            P(("lang", "seq"), None),
            P(("lang", "seq"), None),
            P(("lang", "seq"), None),
            P("lang", "seq", None),
            P("lang", "seq", None),
            P("lang", None, "seq"),
            P(None, None, "seq"),
            P("lang"),
            P("lang", "seq", None),
            P("lang", "seq", None),
            P("lang", "seq", None),
            P("lang", "seq", None),
        ),
        out_specs=(P("lang", "seq", None), P(None, "lang", "seq", None), P(None, None, "seq")),
        check_vma=False,
    )
```

```python
import math

import jax
import jax.numpy as jnp
from jax import lax
from jax.experimental import pallas as pl
from jax.experimental.pallas import tpu as pltpu
from jax.sharding import PartitionSpec as P

HD = 128
MESH = pl.DeviceIdType.MESH
ANY = pl.BlockSpec(memory_space=pl.ANY)
BF = jnp.bfloat16
F32 = jnp.float32
DMA = pltpu.SemaphoreType.DMA
ZN = 4
CHUNKS = 2
YN = 4


def push(src, dst, ssem, rsem, axis, target):
    return pltpu.make_async_remote_copy(
        src_ref=src,
        dst_ref=dst,
        send_sem=ssem,
        recv_sem=rsem,
        device_id={axis: target},
        device_id_type=MESH,
    )


def greet(axes):
    pl.semaphore_wait(pltpu.get_barrier_semaphore(), greet_all(axes))


def greet_all(axes):
    barrier = pltpu.get_barrier_semaphore()
    total = 0
    for axis in axes:
        count, of = everyone(axis)()

        def one(j, carry):
            pl.semaphore_signal(barrier, inc=1, device_id={axis: of(j)}, device_id_type=MESH)
            return carry

        lax.fori_loop(1, count, one, 0)
        total += count - 1
    return total


def everyone(axis):
    def make():
        n = lax.axis_size(axis)
        me = lax.axis_index(axis)
        return n, lambda j: lax.rem(me + j, n)

    return make


def ring_places():
    s = lax.axis_index("seq")
    y, z = lax.div(s, ZN), lax.rem(s, ZN)
    up = lax.rem(y + 1, YN) * ZN + z
    down = lax.rem(y + YN - 1, YN) * ZN + z
    return s, y, z, up, down


def gather_sems(chunks):
    return [DMA((chunks, ZN))] * 11


def gather_steps(source, view, sems):
    zl, zr, zin, us, ur, ds, dr, fus, fur, fds, fdr = sems
    s, y, z, up, down = ring_places()
    low_y = lax.rem(y + YN - 1, YN)
    high_y = lax.rem(y + 1, YN)

    def along(c, col, to_right, own):
        shard = y * ZN + col
        return push(
            source(c) if own else view(c, shard, None),
            view(c, shard, None),
            (zr if to_right else zl).at[c, col],
            zin.at[c, col],
            "seq",
            s + 1 if to_right else s - 1,
        )

    def across(c, col, own):
        shard = y * ZN + col
        src = source(c) if own else view(c, shard, None)
        dst = view(c, shard, None)
        return (
            push(src, dst, us.at[c, col], ur.at[c, col], "seq", up),
            push(src, dst, ds.at[c, col], dr.at[c, col], "seq", down),
        )

    def forwards(c, col):
        low = view(c, low_y * ZN + col, 0)
        high = view(c, high_y * ZN + col, 1)
        return (
            push(low, low, fus.at[c, col], fur.at[c, col], "seq", up),
            push(high, high, fds.at[c, col], fdr.at[c, col], "seq", down),
        )

    def pass_on(c, col):
        go_up, go_down = across(c, col, False)
        first, second = forwards(c, col)
        go_up.wait_recv()
        first.start()
        go_down.wait_recv()
        second.start()

    def each_side(t, do):
        @pl.when(z >= t)
        def _():
            do(z - t, True)

        @pl.when(z + t <= ZN - 1)
        def _():
            do(z + t, False)

    def on_way(to_right, do):
        @pl.when(z < ZN - 1 if to_right else z > 0)
        def _():
            do()

    def begin(c):
        for to_right in (True, False):
            on_way(to_right, lambda: along(c, z, to_right, True).start())
        for copy in across(c, z, True):
            copy.start()

    def step(c, t):
        def arrive(col, to_right):
            along(c, col, to_right, False).wait_recv()
            on_way(to_right, lambda: along(c, col, to_right, False).start())
            for copy in across(c, col, False):
                copy.start()

        each_side(t, arrive)

    def relay(c, t):
        if t == 0:
            pass_on(c, z)
        else:
            each_side(t, lambda col, to_right: pass_on(c, col))

    def landed(c):
        for col in range(ZN):
            for copy in forwards(c, col):
                copy.wait_recv()

    def finish(c):
        for col in range(ZN):
            for copy in across(c, col, False) + forwards(c, col):
                copy.wait_send()
        for to_right in (True, False):
            on_way(to_right, lambda: along(c, z, to_right, True).wait_send())
        for t in range(1, ZN):
            each_side(
                t,
                lambda col, to_right: on_way(
                    to_right, lambda: along(c, col, to_right, False).wait_send()
                ),
            )

    return begin, step, relay, landed, finish


def swap_steps(axis, pieces, send, recv):
    n = lax.axis_size(axis)
    me = lax.axis_index(axis)

    def copy(i, j):
        target = lax.rem(me + j, n)
        source, landing = pieces[i]
        return push(source(target), landing(me), send.at[i, j], recv.at[i, j], axis, target)

    def begin():
        def one(j, carry):
            for i in range(len(pieces)):
                copy(i, j).start()
            return carry

        lax.fori_loop(1, n, one, 0)

    def finish():
        def one(j, carry):
            for i in range(len(pieces)):
                copy(i, j).wait()
            return carry

        lax.fori_loop(1, n, one, 0)

    return begin, finish


def latent_pieces(pairs):
    part = pairs[0][0].shape[1]

    def source(array):
        return lambda t: array.at[:, :, pl.ds(pl.multiple_of(t * HD, HD), HD)]

    def landing(array):
        return lambda m: array.at[:, pl.ds(pl.multiple_of(m * part, part), part), :]

    return [(source(a), landing(b)) for a, b in pairs]


def route(ids, gates, prompt_rows, masks, gate_columns, outgoing):
    experts, capacity, width = outgoing.shape
    count = prompt_rows.shape[0]
    expert = lax.broadcasted_iota(jnp.int32, (experts, count), 0)
    chosen = [expert == ids[k : k + 1, :] for k in range(2)]
    named = jnp.where(jnp.logical_or(chosen[0], chosen[1]), 1.0, 0.0).astype(BF)
    ahead = lax.broadcasted_iota(jnp.int32, (count, count), 0)
    ahead = ahead < lax.broadcasted_iota(jnp.int32, (count, count), 1)
    ahead = jnp.where(ahead, 1.0, 0.0).astype(BF)
    earlier = jnp.dot(named, ahead, preferred_element_type=F32)
    slot = lax.broadcasted_iota(jnp.int32, (experts * capacity, count), 0)
    both = jnp.zeros((experts * capacity, count), F32)
    for k in range(2):
        order = jnp.sum(jnp.where(chosen[k], earlier, 0.0), axis=0, keepdims=True)
        target = ids[k : k + 1, :] * capacity + order.astype(jnp.int32)
        mask = jnp.where(slot == target, 1.0, 0.0)
        masks[k] = mask.astype(BF)
        both = both + mask
        gate_columns[k] = jnp.broadcast_to(gates[k : k + 1, :], (count, count)).T
    both = both.astype(BF)
    tile = 512
    for i in range(width // tile):
        columns = pl.ds(i * tile, tile)
        sent = jnp.dot(both, prompt_rows[:, columns], preferred_element_type=F32)
        outgoing[:, :, columns] = sent.reshape(experts, capacity, tile).astype(BF)


def encode(
    w_parts, prompt_rows, ids, gates, w_kv, latents, heads, kv, rows, kv_sum,
    w_flat, masks, gate_columns, outgoing, whole, arrived, tokens, gate_up, hidden, results, returned, mixed,
    dsend, drecv, rsend, rrecv, lsend, lrecv, own_sem, wsems, msems,
):
    s = lax.axis_index("seq")
    me = lax.axis_index("lang")
    count, width = mixed.shape
    size = w_parts[0].shape[0]
    wide = width // CHUNKS
    experts, capacity, _ = arrived.shape

    def wview(c, shard, half):
        columns = pl.ds(pl.multiple_of(shard * HD, HD), HD)
        if half is None:
            return whole.at[pl.ds(c * size, size), columns]
        part = size // 2
        return whole.at[pl.ds(c * size + half * part, part), columns]

    def mview(c, shard, half):
        columns = pl.ds(c * wide, wide)
        if half is None:
            return rows.at[pl.ds(pl.multiple_of(shard * count, count), count), columns]
        part = count // 2
        at = pl.multiple_of(shard * count + half * part, part)
        return rows.at[pl.ds(at, part), columns]

    wbegin, wstep, wrelay, wlanded, wfinish = gather_steps(lambda c: w_parts[c], wview, wsems)
    begin, step, relay, landed, finish = gather_steps(
        lambda c: mixed.at[:, pl.ds(c * wide, wide)], mview, msems
    )
    dbegin, dfinish = swap_steps(
        "lang", [(lambda t: outgoing.at[t], lambda m: arrived.at[m])], dsend, drecv
    )
    pieces = latent_pieces(list(zip(latents, heads)))
    swaps = [
        swap_steps("seq", [pieces[i]], lsend.at[pl.ds(i, 1)], lrecv.at[pl.ds(i, 1)])
        for i in range(4)
    ]

    def back(c):
        columns = pl.ds(c * wide, wide)
        return swap_steps(
            "lang",
            [(lambda t: results.at[t, :, columns], lambda m: returned.at[m, :, columns])],
            rsend.at[pl.ds(c, 1)],
            rrecv.at[pl.ds(c, 1)],
        )

    backs = [back(c) for c in range(CHUNKS)]
    own = [pltpu.make_async_copy(outgoing.at[me], arrived.at[me], own_sem.at[0])]
    for c in range(3):
        own.append(pltpu.make_async_copy(w_parts[c], wview(c, s, None), own_sem.at[1 + c]))
    for i, (a, b) in enumerate(pieces):
        own.append(pltpu.make_async_copy(a(s), b(s), own_sem.at[4 + i]))
    for c in range(3):
        wbegin(c)
    for copy in own[1:]:
        copy.start()
    route(ids, gates, prompt_rows, masks, gate_columns, outgoing)
    own[0].start()
    for t in range(1, ZN):
        for c in range(3):
            wstep(c, t)
            wrelay(c, t - 1)
        if t == 1:
            dbegin()
        if t == 2:
            swaps[0][0]()
        if t == ZN - 1:
            swaps[1][0]()
            swaps[2][0]()
    for c in range(3):
        wrelay(c, ZN - 1)

    def one_split(i, carry):
        at = pl.ds(pl.multiple_of(i * 256, 256), 256)
        both = w_kv[at, :, :].astype(F32)
        w_flat[at, pl.ds(0, HD)] = both[:, 0, :].astype(BF)
        w_flat[at, pl.ds(HD, HD)] = both[:, 1, :].astype(BF)
        return carry

    lax.fori_loop(0, width // 256, one_split, 0)
    dfinish()
    for copy in own:
        copy.wait()
    for at in range(CHUNKS):
        columns = pl.ds(at * wide, wide)
        slots = arrived[:, :, columns].astype(F32)
        tokens[:, columns] = slots.reshape(experts * capacity, wide).astype(BF)
    wlanded(0)
    wlanded(1)
    gate_up[...] = jnp.zeros_like(gate_up)
    tile = 512

    def one_depth(i, carry):
        columns = pl.ds(pl.multiple_of(i * tile, tile), tile)
        gate_up[...] += lax.dot_general(
            tokens[:, columns],
            whole[pl.ds(0, 2 * size), columns],
            (((1,), (1,)), ((), ())),
            preferred_element_type=F32,
        )
        return carry

    lax.fori_loop(0, width // tile, one_depth, 0)
    gate = gate_up[:, :size]
    hidden[...] = (gate / (1.0 + jnp.exp(-gate)) * gate_up[:, size:]).astype(BF)
    wlanded(2)
    mates = []
    for c in range(CHUNKS):

        def one_tile(i, carry):
            columns = pl.ds(pl.multiple_of(c * wide + i * tile, tile), tile)
            result = jnp.dot(
                hidden[...], whole[pl.ds(2 * size, size), columns], preferred_element_type=F32
            )
            results[:, :, columns] = result.reshape(experts, capacity, tile).astype(BF)
            return carry

        lax.fori_loop(0, wide // tile, one_tile, 0)
        backs[c][0]()
        columns = pl.ds(c * wide, wide)
        mates.append(
            pltpu.make_async_copy(
                results.at[me, :, columns], returned.at[me, :, columns], own_sem.at[c]
            )
        )
        mates[-1].start()
    places = []

    def mix(c):
        backs[c][1]()
        mates[c].wait()
        columns = pl.ds(c * wide, wide)
        slots = returned[:, :, columns].astype(F32)
        slots = slots.reshape(experts * capacity, wide).astype(BF)
        total = jnp.zeros((count, wide), F32)
        for which in range(masks.shape[0]):
            picked = lax.dot_general(
                masks[which], slots, (((0,), (0,)), ((), ())), preferred_element_type=F32
            )
            total = total + gate_columns[which][:, 0:1] * picked
        mixed[:, columns] = total.astype(BF)
        place = pltpu.make_async_copy(
            mixed.at[:, columns], mview(c, s, None), own_sem.at[CHUNKS + c]
        )
        place.start()
        places.append(place)
        begin(c)

    for tick in range(CHUNKS + ZN):
        if tick < CHUNKS:
            mix(tick)
        for c in range(CHUNKS):
            if 0 <= tick - c - 1 < ZN:
                relay(c, tick - c - 1)
        for c in range(CHUNKS):
            if 1 <= tick - c + 1 < ZN:
                step(c, tick - c + 1)
        if tick == CHUNKS + 1:
            swaps[3][0]()
    for copy in places:
        copy.wait()
    for c in range(CHUNKS):
        landed(c)

        def one_part(i, carry):
            at = pl.ds(pl.multiple_of(i * 256, 256), 256)
            depth = pl.ds(c * wide, wide)
            part = jnp.dot(rows[at, depth], w_flat[depth, :], preferred_element_type=F32)
            if c > 0:
                part = part + kv_sum[at, :]
            if c < CHUNKS - 1:
                kv_sum[at, :] = part
            else:
                kv[at, :] = part.astype(BF)
            return carry

        lax.fori_loop(0, rows.shape[0] // 256, one_part, 0)
    for swap in swaps:
        swap[1]()
    for c in range(3):
        wfinish(c)
    for c in range(CHUNKS):
        finish(c)


def whole_kernel(*refs):
    refs = list(refs)

    def take(n):
        got = refs[:n]
        del refs[:n]
        return got

    (lengths, ids, gates, w_kv, prompt_rows) = take(5)
    w_parts = take(3)
    latents = take(4)
    outs = take(3)
    heads = take(4)
    kv, rows = take(2)
    encode_scratch = take(12)
    encode_sems = take(7)
    wsems = take(11)
    msems = take(11)
    greet(["seq", "lang"])
    encode(
        w_parts, prompt_rows, ids, gates, w_kv, latents, heads, kv, rows, refs[9],
        *encode_scratch, *encode_sems, wsems, msems,
    )
    q, k, v, g = heads
    attend(lengths, q, g, k, v, kv, rows, *outs, *refs)


def attend(
    lengths, q_ref, g_ref, k_ref, v_ref, kv_ref, rows, att_rows, latent, total,
    att, qg, kg, vg, pg_t, kt, vt, kacc, vacc, e_s, d_s,
    outbound, parts, mine, pair, done,
    send, recv, own_sem, rsend, rrecv, psend, precv, asend, arecv,
):
    s = lax.axis_index("seq")
    l = lax.axis_index("lang")
    n = lax.axis_size("seq")
    y = lax.div(s, ZN)
    group = lax.axis_size("lang") // 2
    high, j = lax.div(l, group), lax.rem(l, group)
    pages, lat, _ = q_ref.shape
    part = att_rows.shape[1]
    chunk = rows.shape[1] // group
    sources = [att, qg, kg, vg]
    landings = [att_rows, latent.at[0], latent.at[1], latent.at[2]]

    def out(i, page, to, frm):
        return push(
            sources[i].at[page, pl.ds(pl.multiple_of(to * part, part), part), :],
            landings[i].at[page, :, pl.ds(pl.multiple_of(frm * HD, HD), HD)],
            send.at[i, page, to],
            recv.at[i, page, frm],
            "seq",
            to,
        )

    step = 256
    blocks = YN
    bq = lat // blocks
    keys_all = 2 * lat
    steps = keys_all // step
    scale = 1.0 / math.sqrt(HD)
    to_two = scale * math.log2(math.e)
    nt = (((1,), (1,)), ((), ()))

    def one_block(turn, carry):
        page, at_block = lax.div(turn, blocks), lax.rem(turn, blocks)
        block = lax.rem(y + 1 + at_block, blocks)
        length = jnp.where(page == 0, lengths[0], lengths[1])

        def key_part(i):
            at = i * step
            if at < lat:
                return k_ref[page, pl.ds(at, step), :]
            return kv_ref[pl.ds(pl.multiple_of(page * lat + at - lat, step), step), pl.ds(0, HD)]

        def value_part(i):
            at = i * step
            if at < lat:
                return v_ref[page, pl.ds(at, step), :]
            return kv_ref[pl.ds(pl.multiple_of(page * lat + at - lat, step), step), pl.ds(HD, HD)]

        @pl.when(at_block == 0)
        def _():
            for i in range(steps):
                kt[:, pl.ds(i * step, step)] = key_part(i).T
                vt[:, pl.ds(i * step, step)] = value_part(i).T
            kacc[...] = jnp.zeros_like(kacc)
            vacc[...] = jnp.zeros_like(vacc)

        places = pl.ds(pl.multiple_of(block * bq, bq), bq)
        q, g = q_ref[page, places, :], g_ref[page, places, :]
        highest = jnp.full((1, bq), -jnp.inf, F32)
        for i in range(steps):
            scores = lax.dot_general(key_part(i), q, nt, preferred_element_type=F32)
            if i * step >= lat:
                at = i * step - lat + lax.broadcasted_iota(jnp.int32, (step, bq), 0)
                scores = jnp.where(at < length, scores, -jnp.inf)
            highest = jnp.maximum(highest, jnp.max(scores, axis=0, keepdims=True))
            e_s[pl.ds(i * step, step), :] = scores
        top = highest * to_two
        weight = jnp.zeros((1, bq), F32)
        weighted = jnp.zeros((1, bq), F32)
        for i in range(steps):
            raised = jnp.exp2(e_s[pl.ds(i * step, step), :] * to_two - top)
            prob_grad = lax.dot_general(value_part(i), g, nt, preferred_element_type=F32)
            weight = weight + jnp.sum(raised, axis=0, keepdims=True)
            weighted = weighted + jnp.sum(raised * prob_grad, axis=0, keepdims=True)
            e_s[pl.ds(i * step, step), :] = raised
            d_s[pl.ds(i * step, step), :] = prob_grad
        inverse = 1.0 / weight
        centre = weighted * inverse
        scaled = inverse * scale
        att_t = jnp.zeros((HD, bq), F32)
        qg_t = jnp.zeros((HD, bq), F32)
        for i in range(steps):
            at = pl.ds(i * step, step)
            raised = e_s[at, :]
            soft_low = (raised * inverse).astype(BF)
            score_grad = (raised * scaled * (d_s[at, :] - centre)).astype(BF)
            att_t = att_t + jnp.dot(vt[:, at], soft_low, preferred_element_type=F32)
            qg_t = qg_t + jnp.dot(kt[:, at], score_grad, preferred_element_type=F32)
            vacc[at, :] += jnp.dot(soft_low, g, preferred_element_type=F32)
            kacc[at, :] += jnp.dot(score_grad, q, preferred_element_type=F32)
        att[page, places, :] = att_t.T.astype(BF)
        qg[page, places, :] = qg_t.T.astype(BF)
        for z in range(ZN):
            to = block * ZN + z

            @pl.when(to != s)
            def _():
                out(0, page, to, s).start()
                out(1, page, to, s).start()

        @pl.when(at_block == blocks - 1)
        def _():
            kg[page] = kacc[pl.ds(0, lat), :].astype(BF)
            vg[page] = vacc[pl.ds(0, lat), :].astype(BF)
            columns = pl.ds(pl.multiple_of(page * lat, lat), lat)
            pg_t[pl.ds(0, HD), columns] = kacc[pl.ds(lat, lat), :].T.astype(BF)
            pg_t[pl.ds(HD, HD), columns] = vacc[pl.ds(lat, lat), :].T.astype(BF)

            @pl.when(page < pages - 1)
            def _():
                send_key_grads(page)

        return carry

    def send_key_grads(page):
        def one(k, carry):
            to = lax.rem(s + k, n)
            out(2, page, to, s).start()
            out(3, page, to, s).start()
            return carry

        lax.fori_loop(1, n, one, 0)

    lax.fori_loop(0, pages * blocks, one_block, 0)

    def mate(k):
        return high * group + lax.rem(j + k, group)

    def summed(t):
        columns = pl.ds(pl.multiple_of(t * chunk, chunk), chunk)
        return jnp.dot(pg_t[...], rows[:, columns], preferred_element_type=F32)

    def scatter(k):
        return push(
            outbound.at[k], parts.at[group - k], rsend.at[k], rrecv.at[k], "lang", mate(k)
        )

    def piece(t):
        return total.at[pl.ds(pl.multiple_of(t * chunk, chunk), chunk), :]

    def spread(k, t):
        return push(done, piece(t), asend.at[k], arecv.at[k], "lang", mate(k))

    def one_part(k, carry):
        outbound[k] = summed(lax.rem(j + k, group)).astype(BF)
        scatter(k).start()
        return carry

    lax.fori_loop(1, group, one_part, 0)
    own = []
    for i in range(4):
        own.append(
            pltpu.make_async_copy(
                sources[i].at[:, pl.ds(pl.multiple_of(s * part, part), part), :],
                landings[i].at[:, :, pl.ds(pl.multiple_of(s * HD, HD), HD)],
                own_sem.at[i],
            )
        )
        own[-1].start()
    acc = summed(j)
    for k in range(1, group):
        scatter(k).wait()
        acc = acc + parts[group - k].astype(F32)
    mine[...] = acc.astype(BF)
    cross = push(
        mine, pair, psend.at[0], precv.at[0], "lang", lax.rem(l + group, 2 * group)
    )
    cross.start()
    send_key_grads(pages - 1)
    cross.wait()
    done[...] = (mine[...].astype(F32) + pair[...].astype(F32)).T.astype(BF)
    for k in range(1, group):
        spread(k, j).start()
    last = pltpu.make_async_copy(done, piece(j), own_sem.at[4])
    last.start()

    def ended(k, carry):
        other = lax.rem(s + k, n)
        for i in range(4):
            for page in range(pages):
                out(i, page, other, other).wait()
        return carry

    lax.fori_loop(1, n, ended, 0)
    for copy in own:
        copy.wait()
    last.wait()
    for k in range(1, group):
        spread(k, lax.rem(j + group - k, group)).wait()


def remote(body, number, out_shape, scratch, *operands, in_vmem=(), in_smem=()):
    return pl.pallas_call(
        body,
        out_shape=out_shape,
        in_specs=[
            pl.BlockSpec(memory_space=pltpu.SMEM)
            if i in in_smem
            else pl.BlockSpec(memory_space=pltpu.VMEM)
            if i in in_vmem
            else ANY
            for i in range(len(operands))
        ],
        out_specs=[ANY] * len(out_shape),
        scratch_shapes=scratch,
        compiler_params=pltpu.CompilerParams(
            collective_id=number, has_side_effects=True, vmem_limit_bytes=60 << 20
        ),
    )(*operands)


def local(
    prompt_rows,
    expert_ids,
    expert_gates,
    w_gate,
    w_up,
    w_down,
    w_kv,
    prompt_lengths,
    latent_q,
    latent_k,
    latent_v,
    grad_out,
):
    lang_count = lax.axis_size("lang")
    seq_count = lax.axis_size("seq")
    experts_all = lang_count
    rows_local, model_width = prompt_rows.shape
    ff = w_gate.shape[2]
    capacity = 3 * rows_local // experts_all
    sds = jax.ShapeDtypeStruct
    pages, part, _ = latent_q.shape
    lat = part * seq_count
    half = lang_count // 2
    chunk = model_width // half
    bq = lat // YN
    slots = experts_all * capacity
    blocks = (experts_all, capacity, model_width)
    att_rows, latent, total = remote(
        whole_kernel,
        1,
        [
            sds(latent_q.shape, BF),
            sds((3,) + latent_q.shape, BF),
            sds((model_width, 2 * HD), BF),
        ],
        [pltpu.VMEM((pages, lat, HD), BF)] * 4
        + [
            pltpu.VMEM((pages * lat, 2 * HD), BF),
            pltpu.VMEM((rows_local * seq_count, model_width), BF),
            pltpu.VMEM((model_width, 2 * HD), BF),
            pltpu.VMEM((2, slots, rows_local), BF),
            pltpu.VMEM((2, rows_local, rows_local), F32),
            pltpu.VMEM(blocks, BF),
            pltpu.VMEM((3 * ff, model_width), BF),
            pltpu.VMEM(blocks, BF),
            pltpu.VMEM((slots, model_width), BF),
            pltpu.VMEM((slots, 2 * ff), F32),
            pltpu.VMEM((slots, ff), BF),
            pltpu.VMEM(blocks, BF),
            pltpu.VMEM(blocks, BF),
            pltpu.VMEM((rows_local, model_width), BF),
            DMA((1, lang_count)),
            DMA((1, lang_count)),
            DMA((CHUNKS, lang_count)),
            DMA((CHUNKS, lang_count)),
            DMA((4, seq_count)),
            DMA((4, seq_count)),
            DMA((8,)),
        ]
        + gather_sems(3)
        + gather_sems(CHUNKS)
        + [pltpu.VMEM((pages, lat, HD), BF)] * 4
        + [
            pltpu.VMEM((2 * HD, pages * lat), BF),
            pltpu.VMEM((HD, 2 * lat), BF),
            pltpu.VMEM((HD, 2 * lat), BF),
            pltpu.VMEM((2 * lat, HD), F32),
            pltpu.VMEM((2 * lat, HD), F32),
            pltpu.VMEM((2 * lat, bq), F32),
            pltpu.VMEM((2 * lat, bq), F32),
            pltpu.VMEM((half, 2 * HD, chunk), BF),
            pltpu.VMEM((half, 2 * HD, chunk), BF),
            pltpu.VMEM((2 * HD, chunk), BF),
            pltpu.VMEM((2 * HD, chunk), BF),
            pltpu.VMEM((chunk, 2 * HD), BF),
            DMA((4, pages, seq_count)),
            DMA((4, pages, seq_count)),
            DMA((5,)),
            DMA((half,)),
            DMA((half,)),
            DMA((1,)),
            DMA((1,)),
            DMA((half,)),
            DMA((half,)),
        ],
        prompt_lengths,
        expert_ids.T,
        expert_gates.T,
        w_kv,
        prompt_rows,
        w_gate[0].T,
        w_up[0].T,
        w_down[0],
        latent_q,
        latent_k,
        latent_v,
        grad_out,
        in_vmem=(1, 2, 3, 4),
        in_smem=(0,),
    )
    grad_wkv = total.astype(F32).reshape(model_width, 2, HD)
    return (att_rows, latent, grad_wkv)


def solution(mesh):
    return jax.shard_map(
        local,
        mesh=mesh,
        in_specs=(
            P(("lang", "seq"), None),
            P(("lang", "seq"), None),
            P(("lang", "seq"), None),
            P("lang", "seq", None),
            P("lang", "seq", None),
            P("lang", None, "seq"),
            P(None, None, "seq"),
            P("lang"),
            P("lang", "seq", None),
            P("lang", "seq", None),
            P("lang", "seq", None),
            P("lang", "seq", None),
        ),
        out_specs=(P("lang", "seq", None), P(None, "lang", "seq", None), P(None, None, "seq")),
        check_vma=False,
    )
```
